256 devices in a mesh: dp: 8 (over x, core), context: 32 (over z, y).
Axes of the slice: x: 4, y: 4, z: 8, core: 2. Of those that a mesh axis runs over, the one named last changes fastest.
Arguments:
- tokens: bfloat16 [8, 8192, 2048], P('dp', 'context'), may hold values from -6 to 6
- weight: bfloat16 [2048, 2048], P('context'), may hold values from -0.125 to 0.125
- gate: bfloat16 [8, 8192, 2048], P('dp', 'context'), may hold values from -6 to 6
- skip: float32 [2048], replicated, may hold values from 0.1 to 1.9
- first_factor: bfloat16 [64, 128, 128], P('context'), may hold values from -0.5 to 0.5
- second_factor: bfloat16 [128, 64, 64], P('context'), may hold values from -0.75 to 0.75
- kernel: bfloat16 [64, 128, 2048], P(None, 'context'), may hold values from -6 to 6
- third_factor: bfloat16 [128, 64, 64], P('context'), may hold values from -0.75 to 0.75
- fourth_factor: bfloat16 [64, 128, 128], P('context'), may hold values from -0.5 to 0.5
- cotangent: bfloat16 [8, 8192, 2048], P('dp', 'context'), may hold values from -6 to 6
Outputs:
- mixed: bfloat16 [8, 8192, 2048], P('dp', 'context')
- grad_tokens: bfloat16 [8, 8192, 2048], P('dp', 'context')
- grad_gate: bfloat16 [8, 8192, 2048], P('dp', 'context')
- grad_weight: float32 [2048, 2048], P('context')
The draws below stay inside these ranges and needn't reach their ends.
All inputs are finite; a program needn't handle non-finite values.
Results may differ from the reference program's by a relative error of at most 0.019.
Values may be sent and summed in bfloat16 or wider, within the bound.
A program may use at most 128 MiB of HBM per device.

```python
import jax
import jax.numpy as jnp
from jax import lax

D = 2048
R = 128
TOK_DEV = 256
SEQS = 8
N = 8192
Q = 64
N_CONTEXT = 32


def strengthened(entries, rng, source, target, parts, factor):
    def block_of(dim):
        return (jnp.arange(entries.shape[dim]) // (entries.shape[dim] // parts)).reshape((-1,) + (1,) * (entries.ndim - 1 - dim))

    near = jax.random.permutation(rng, parts)[block_of(target)]
    other_side = (block_of(target) + parts // 2) % parts
    return jnp.where((block_of(source) == near) | (block_of(source) == other_side), factor * entries, entries)


def block_levels(rng, extent, split, least, high):
    loudness, own = 1.0, jax.random.fold_in(rng, 6)
    for dim, shards_of in split:
        draws = jnp.exp(jax.random.uniform(jax.random.fold_in(own, dim), (shards_of,), jnp.float32, least / len(split), high / len(split)))
        loudness = loudness * jnp.repeat(draws, extent[dim] // shards_of).reshape([-1 if axis == dim else 1 for axis in range(len(extent))])
    return loudness


def scatter_about(key, shape, scale, most, shards=(), kind=jnp.bfloat16):
    values = scale * jax.random.normal(key, shape, jnp.float32)
    if shards:
        values = values * block_levels(key, shape, shards, -0.22, 0.18)
    return jnp.clip(values, -most, most).astype(kind)


def noise_with(own_key, extent, spread, limit, cuts, heavy, kind=jnp.bfloat16):
    drawn = spread * jax.random.normal(own_key, extent, jnp.float32)
    if cuts:
        drawn = drawn * block_levels(own_key, extent, cuts, -0.22, 0.18)
    return jnp.clip(strengthened(drawn, jax.random.fold_in(own_key, 3), *heavy), -limit, limit).astype(kind)


def setup_inputs(seed: int = 0) -> dict:
    seeds = jax.random.split(jax.random.key(seed), 11)
    tokens = noise_with(seeds[0], (SEQS, N, D), 1.0, 6.0, ((0, 8), (1, 32)), (1, 2, 32, 2.75))
    weight = scatter_about(seeds[1], (D, D), D ** -0.5, 0.125, ((0, 32),))
    gate = scatter_about(seeds[2], (SEQS, N, D), 1.0, 6.0, ((0, 8), (1, 32)))
    skip = jnp.clip(1.0 + 0.18 * jax.random.normal(seeds[3], (D,), jnp.float32), 0.1, 1.9)
    first_factor = scatter_about(seeds[4], (Q, R, R), R ** -0.5, 0.5, ((0, 32),))
    second_factor = scatter_about(seeds[5], (R, Q, Q), Q ** -0.5, 0.75, ((0, 32),))
    kernel = scatter_about(seeds[6], (Q, R, D), 1.0, 6.0, ((1, 32),))
    third_factor = scatter_about(seeds[7], (R, Q, Q), Q ** -0.5, 0.75, ((0, 32),))
    fourth_factor = scatter_about(seeds[8], (Q, R, R), R ** -0.5, 0.5, ((0, 32),))
    cotangent = scatter_about(seeds[9], (SEQS, N, D), 1.0, 6.0, ((0, 8), (1, 32)))
    return {"tokens": tokens, "weight": weight, "gate": gate, "skip": skip, "first_factor": first_factor, "second_factor": second_factor, "kernel": kernel, "third_factor": third_factor, "fourth_factor": fourth_factor, "cotangent": cotangent}


def widen(value):
    return value.astype(jnp.float32)


def reference(tokens, weight, gate, skip, first_factor, second_factor, kernel, third_factor, fourth_factor, cotangent):
    fac_one = widen(first_factor)
    fac_two = widen(second_factor)
    fac_three = widen(third_factor)
    fac_four = widen(fourth_factor)
    kern = widen(kernel)

    def one_sequence(total, inputs):
        seq_tokens, seq_gate, seq_grad = inputs
        proj = jnp.dot(seq_tokens, weight, preferred_element_type=jnp.float32).astype(jnp.bfloat16)
        proj_blocks = widen(proj).reshape(Q, R, D)
        first_mix = jnp.einsum('qsr,qrc->qsc', fac_one, proj_blocks).astype(jnp.bfloat16)
        second_mix = jnp.einsum('stq,qsc->tsc', fac_two, widen(first_mix))
        filtered = (second_mix * kern).astype(jnp.bfloat16)
        third_mix = jnp.einsum('spt,tsc->psc', fac_three, widen(filtered)).astype(jnp.bfloat16)
        field = jnp.einsum('qrs,qsc->qrc', fac_four, widen(third_mix)).reshape(N, D)
        pre_gate = field + skip * widen(proj)
        gate_vals = widen(seq_gate)
        out_grad = widen(seq_grad)
        mixed = (gate_vals * pre_gate).astype(jnp.bfloat16)
        grad_gate = (out_grad * pre_gate).astype(jnp.bfloat16)
        gated_grad = (out_grad * gate_vals).astype(jnp.bfloat16)
        grad_third = jnp.einsum('qrs,qrc->qsc', fac_four, widen(gated_grad).reshape(Q, R, D)).astype(jnp.bfloat16)
        grad_filtered_in = jnp.einsum('spt,psc->tsc', fac_three, widen(grad_third))
        grad_second = (grad_filtered_in * kern).astype(jnp.bfloat16)
        grad_first = jnp.einsum('stq,tsc->qsc', fac_two, widen(grad_second)).astype(jnp.bfloat16)
        grad_field = jnp.einsum('qsr,qsc->qrc', fac_one, widen(grad_first)).reshape(N, D)
        grad_proj = (grad_field + skip * widen(gated_grad)).astype(jnp.bfloat16)
        grad_tokens = jnp.dot(grad_proj, weight.T, preferred_element_type=jnp.float32).astype(jnp.bfloat16)
        token_runs = seq_tokens.reshape(N_CONTEXT, TOK_DEV, D)
        grad_runs = grad_proj.reshape(N_CONTEXT, TOK_DEV, D)

        def add_run(running, block_pair):
            partial_value = jnp.dot(block_pair[0].T, block_pair[1], preferred_element_type=jnp.float32).astype(jnp.bfloat16)
            return running + widen(partial_value), None

        total, _ = lax.scan(add_run, total, (token_runs, grad_runs))
        return total, (mixed, grad_tokens, grad_gate)

    start_total = jnp.zeros((D, D), jnp.float32)
    grad_weight, outputs = lax.scan(one_sequence, start_total, (tokens, gate, cotangent))
    return outputs[0], outputs[1], outputs[2], grad_weight
```

```python
import functools

import jax
import jax.numpy as jnp
from jax import lax
from jax.experimental import pallas as pl
from jax.experimental.pallas import tpu as pltpu
from jax.sharding import PartitionSpec as P

BF = jnp.bfloat16
F32 = jnp.float32
MESH = pl.DeviceIdType.MESH
X = 4
NC = 2


def mm(a, b):
    return jnp.dot(a, b, preferred_element_type=F32)


def mm_ta(a, b):
    return lax.dot_general(a, b, (((0,), (0,)), ((), ())), preferred_element_type=F32)


def mm_tb(a, b):
    return lax.dot_general(a, b, (((1,), (1,)), ((), ())), preferred_element_type=F32)


def iota(shape, dim):
    return lax.broadcasted_iota(jnp.int32, shape, dim)


def ones_where(cond):
    return jnp.where(cond, 1.0, 0.0).astype(BF)


def loop(lo, hi, body):
    lax.fori_loop(lo, hi, lambda i, c: (body(i), c)[1], 0)


def kernel(
    Y,
    tok, wgt, gate, skip, f1, f2, kern, f3, f4, cot,
    mixed, gtok, ggate, gwt,
    tother, g, gx, gp, p, wb, gw, sb, rb, rxa, rxc, sx, ry, sy, rz, fin, gfin,
    a1, a2, a3t, a4t, u, gts, gtr, pgs, pgr, pgo,
    s_ag, r_ag, s_pair, r_pair, s_a2a, r_a2a, s_rs, r_rs,
):
    dp = lax.axis_index("dp")
    k = lax.axis_index("context")
    DP = 2 * X
    Z = wb.shape[0]
    CTX = Z * Y
    h, x = lax.rem(dp, 2), lax.div(dp, 2)
    z, y = lax.div(k, Y), lax.rem(k, Y)
    right, left = lax.rem(x + 1, X), lax.rem(x + X - 1, X)
    opp = lax.rem(x + 2, X)
    other = 1 - h
    pair = x * 2 + other
    rows, D = tok.shape
    HC = D // 2
    QL, R = f1.shape[0], f1.shape[1]
    SL, Q = f2.shape[0], f2.shape[1]
    M = 2 * rows
    CH = M // CTX
    CW = HC // NC
    WR = wb.shape[3]
    half = pl.multiple_of(h * HC, HC)
    ohalf = pl.multiple_of(other * HC, HC)
    ZH = Z // 2
    TI = D // Z

    def remote(src, dst, ss, rs, dev):
        return pltpu.make_async_remote_copy(
            src_ref=src, dst_ref=dst, send_sem=ss, recv_sem=rs, device_id=dev, device_id_type=MESH
        )

    EB = 32

    def gate_rows(i):
        r = pl.ds(pl.multiple_of(i * EB, EB), EB)
        g[h, r, :] = (cot[r, pl.ds(half, HC)].astype(F32) * gate[r, pl.ds(half, HC)].astype(F32)).astype(BF)
        gx[r, :] = (cot[r, pl.ds(ohalf, HC)].astype(F32) * gate[r, pl.ds(ohalf, HC)].astype(F32)).astype(BF)

    loop(0, rows // EB, gate_rows)

    barrier = pltpu.get_barrier_semaphore()

    def greet_context(d):
        pl.semaphore_signal(barrier, inc=1, device_id=(dp, lax.rem(k + d, CTX)), device_id_type=MESH)

    def greet_dp(d):
        pl.semaphore_signal(barrier, inc=1, device_id=(lax.rem(dp + d, DP), k), device_id_type=MESH)

    loop(1, CTX, greet_context)
    loop(1, DP, greet_dp)
    pl.semaphore_wait(barrier, CTX - 1 + DP - 1)

    c_g = remote(gx, g.at[h], s_pair.at[0], r_pair.at[0], (pair, k))
    c_g.start()

    def ag_z(d):
        zz = lax.rem(z + d, Z)
        remote(
            wgt.at[x, :, pl.ds(half, HC)], wb.at[z, y, x], s_ag.at[0], r_ag.at[0], (dp, zz * Y + y)
        ).start()

    loop(1, Z, ag_z)
    c_tok = remote(tok, tother, s_pair.at[1], r_pair.at[1], (pair, k))
    c_tok.start()
    wb[z, y, x] = wgt[x, :, pl.ds(half, HC)]

    def row_matrix(dst, factor, transposed):
        rr, ss = iota((M, R), 0), iota((M, R), 1)
        for b in range(2):
            for q in range(QL):
                e = ones_where(rr == (ss // SL) * CH + b * (QL * SL) + q * SL + ss % SL)
                block = mm_tb(e, factor[q]) if transposed else mm(e, factor[q])
                dst[:, (b * QL + q) * R:(b * QL + q + 1) * R] = block.astype(BF)

    def column_matrix(dst, factor, transposed):
        qq, cc = iota((Q, M), 0), iota((Q, M), 1)
        for s in range(SL):
            e = ones_where(
                (cc // CH == qq // QL) & ((cc // SL) % QL == qq % QL) & (cc % SL == s)
            )
            block = mm_ta(factor[s], e) if transposed else mm(factor[s], e)
            u[s * Q:(s + 1) * Q, :] = block.astype(BF)
        rr, cc = iota((Q * SL, SL * Q), 0), iota((Q * SL, SL * Q), 1)
        move = ones_where((rr // SL == cc % Q) & (rr % SL == cc // Q))
        full = mm(move, u[...])
        owner = (iota((Q * SL, M), 1) // (QL * SL)) % 2
        for b in range(2):
            dst[b * Q * SL:(b + 1) * Q * SL, :] = jnp.where(owner == b, full, 0.0).astype(BF)

    row_matrix(a4t, f4, True)
    column_matrix(a3t, f3, True)

    def a2a_start(ph, c):
        def send(d):
            kk = lax.rem(k + d, CTX)
            remote(
                sb.at[ph, c, kk], rb.at[ph, c, k], s_a2a.at[ph, c], r_a2a.at[ph, c], (dp, kk)
            ).start()

        loop(1, CTX, send)
        rb[ph, c, k] = sb[ph, c, k]

    def a2a_desc(ph, c):
        most = pl.ds(0, CTX - 1)
        return remote(
            sb.at[ph, c, most], rb.at[ph, c, most], s_a2a.at[ph, c], r_a2a.at[ph, c],
            (dp, lax.rem(k + 1, CTX)),
        )

    def put(ph, c, value):
        sb[ph, c] = value.astype(BF).reshape(CTX, CH, CW)

    def got(ph, c):
        return rb[ph, c].reshape(M, CW)

    def cols(c):
        return slice(c * CW, (c + 1) * CW)

    c_g.wait_recv()
    for c in range(NC):
        put(0, c, mm(a4t[...], g[:, :, cols(c)].reshape(M, CW)))
        a2a_start(0, c)

    column_matrix(a2, f2, False)

    zs = pl.ds(0, Z - 1)
    remote(wb.at[zs, y, x], wb.at[zs, y, x], s_ag.at[0], r_ag.at[0], (pair, k)).wait_recv()

    def ag_y(d):
        yy = lax.rem(y + d, Y)
        remote(wb.at[:, y, x], wb.at[:, y, x], s_ag.at[1], r_ag.at[1], (dp, z * Y + yy)).start()

    loop(1, Y, ag_y)
    row_matrix(a1, f1, False)
    ys = pl.ds(0, Y - 1)
    ag_y_desc = remote(wb.at[:, ys, x], wb.at[:, ys, x], s_ag.at[1], r_ag.at[1], (pair, k))
    ag_y_desc.wait_recv()
    rdev, ldev = (right * 2 + h, k), (left * 2 + h, k)
    c_xr = remote(wb.at[:, :, x], wb.at[:, :, x], s_ag.at[2], r_ag.at[2], rdev)
    c_xl = remote(wb.at[:, :, x], wb.at[:, :, x], s_ag.at[3], r_ag.at[3], ldev)
    c_xr.start()
    c_xl.start()

    def kern_of(c):
        return kern[:, pl.ds(pl.multiple_of(h * HC + c * CW, CW), CW)].astype(F32)

    def filtered(value, c):
        kc = kern_of(c)
        return (value.reshape(2, Q * SL, CW) * kc[None]).astype(BF).reshape(M, CW)

    for c in range(NC):
        a2a_desc(0, c).wait_recv()
        gs = filtered(mm(a3t[...], got(0, c)), c)
        put(1, c, mm_ta(a2[...], gs))
        a2a_start(1, c)

    lo, hi = pl.ds(0, ZH), pl.ds(ZH, Z - ZH)
    c_xr.wait_recv()
    c_xr2 = remote(wb.at[lo, :, left], wb.at[lo, :, left], s_ag.at[4], r_ag.at[4], rdev)
    c_xr2.start()
    c_xl.wait_recv()
    c_xl2 = remote(wb.at[hi, :, right], wb.at[hi, :, right], s_ag.at[5], r_ag.at[5], ldev)
    c_xl2.start()
    c_tok.wait_recv()
    c_xr2.wait_recv()
    c_xl2.wait_recv()

    for c in range(NC):
        wc = wb[:, :, :, :, cols(c)].reshape(D, CW)
        p[h, :, cols(c)] = mm(tok[...], wc).astype(BF)
        p[other, :, cols(c)] = mm(tother[...], wc).astype(BF)
        put(2, c, mm(a1[...], p[:, :, cols(c)].reshape(M, CW)))
        a2a_start(2, c)

    def skip_of(c):
        return skip[:, pl.ds(pl.multiple_of(h * HC + c * CW, CW), CW)]

    for c in range(NC):
        a2a_desc(1, c).wait_recv()
        gf = mm_ta(a1[...], got(1, c)) + skip_of(c) * g[:, :, cols(c)].reshape(M, CW).astype(F32)
        gp[:, :, cols(c)] = gf.astype(BF).reshape(2, rows, CW)

    def gw_rows(i):
        at = pl.ds(pl.multiple_of(i * TI, TI), TI)
        part = mm_ta(tok[:, at], gp[h]) + mm_ta(tother[:, at], gp[other])
        gw[i] = part.astype(BF).reshape(Y, X, WR, HC)

    loop(0, Z, gw_rows)
    c_r1 = remote(gw.at[lo, :, opp], rxa.at[0], s_rs.at[0], r_rs.at[0], rdev)
    c_l1 = remote(gw.at[hi, :, opp], rxa.at[1], s_rs.at[1], r_rs.at[1], ldev)
    c_r2 = remote(gw.at[hi, :, right], rxc.at[0, hi], s_rs.at[2], r_rs.at[2], rdev)
    c_l2 = remote(gw.at[lo, :, left], rxc.at[1, lo], s_rs.at[3], r_rs.at[3], ldev)
    for copy in (c_r1, c_l1, c_r2, c_l2):
        copy.start()

    for c in range(NC):
        a2a_desc(2, c).wait_recv()
        fl = filtered(mm(a2[...], got(2, c)), c)
        put(3, c, mm_ta(a3t[...], fl))
        a2a_start(3, c)

    c_r1.wait_recv()

    def add_right(i):
        gw[i, :, right] = (gw[i, :, right].astype(F32) + rxa[0, i].astype(F32)).astype(BF)

    loop(0, ZH, add_right)
    c_r3 = remote(gw.at[lo, :, right], rxc.at[0, lo], s_rs.at[4], r_rs.at[4], rdev)
    c_r3.start()
    c_l1.wait_recv()

    def add_left(i):
        gw[ZH + i, :, left] = (gw[ZH + i, :, left].astype(F32) + rxa[1, i].astype(F32)).astype(BF)

    loop(0, ZH, add_left)
    c_l3 = remote(gw.at[hi, :, left], rxc.at[1, hi], s_rs.at[5], r_rs.at[5], ldev)
    c_l3.start()

    def gt_other(i):
        at = pl.ds(pl.multiple_of(i * TI, TI), TI)
        gts[:, at] = mm_tb(gp[other], wb[i].reshape(TI, HC)).astype(BF)

    loop(0, Z, gt_other)
    c_gt = remote(gts, gtr, s_pair.at[2], r_pair.at[2], (pair, k))
    c_gt.start()

    for copy in (c_r2, c_l2, c_r3, c_l3):
        copy.wait_recv()

    def sum_x(i):
        sx[i] = (gw[i, :, x].astype(F32) + rxc[0, i].astype(F32) + rxc[1, i].astype(F32)).astype(BF)

    loop(0, Z, sum_x)

    def rs_y(d):
        yy = lax.rem(y + d, Y)
        remote(sx.at[:, yy], ry.at[d - 1], s_rs.at[6], r_rs.at[6], (dp, z * Y + yy)).start()

    loop(1, Y, rs_y)
    rs_y_desc = remote(ry, ry, s_rs.at[6], r_rs.at[6], (pair, k))

    c_gt.wait_recv()

    def gt_own(i):
        at = pl.ds(pl.multiple_of(i * TI, TI), TI)
        gtok[:, at] = (mm_tb(gp[h], wb[i].reshape(TI, HC)) + gtr[:, at].astype(F32)).astype(BF)

    loop(0, Z, gt_own)

    rs_y_desc.wait_recv()

    def sum_y(i):
        total = sx[i, y].astype(F32)
        for d in range(Y - 1):
            total = total + ry[d, i].astype(F32)
        sy[i] = total.astype(BF)

    loop(0, Z, sum_y)

    def rs_z(d):
        zz = lax.rem(z + d, Z)
        remote(sy.at[zz], rz.at[d - 1], s_rs.at[7], r_rs.at[7], (dp, zz * Y + y)).start()

    loop(1, Z, rs_z)

    for c in range(NC):
        a2a_desc(3, c).wait_recv()
        pre = mm_ta(a4t[...], got(3, c)) + skip_of(c) * p[:, :, cols(c)].reshape(M, CW).astype(F32)
        pgo[:, :, cols(c)] = pre.astype(BF).reshape(2, rows, CW)
    c_pg = remote(pgo.at[other], pgr, s_pair.at[3], r_pair.at[3], (pair, k))
    c_pg.start()

    rs_z_desc = remote(rz, rz, s_rs.at[7], r_rs.at[7], (pair, k))
    rs_z_desc.wait_recv()
    total = sy[z].astype(F32)
    for d in range(Z - 1):
        total = total + rz[d].astype(F32)
    fin[...] = total.astype(BF)

    def share(d):
        remote(
            fin, gfin.at[dp], s_rs.at[8], r_rs.at[8], (lax.rem(dp + d, DP), k)
        ).start()

    loop(1, DP, share)
    gfin[dp] = fin[...]

    def gate_out(i):
        r = pl.ds(pl.multiple_of(i * EB, EB), EB)
        own = pgo[h, r, :].astype(F32)
        mixed[r, pl.ds(half, HC)] = (gate[r, pl.ds(half, HC)].astype(F32) * own).astype(BF)
        ggate[r, pl.ds(half, HC)] = (cot[r, pl.ds(half, HC)].astype(F32) * own).astype(BF)

    loop(0, rows // EB, gate_out)
    c_pg.wait_recv()

    def gate_out_other(i):
        r = pl.ds(pl.multiple_of(i * EB, EB), EB)
        got_pre = pgr[r, :].astype(F32)
        mixed[r, pl.ds(ohalf, HC)] = (gate[r, pl.ds(ohalf, HC)].astype(F32) * got_pre).astype(BF)
        ggate[r, pl.ds(ohalf, HC)] = (cot[r, pl.ds(ohalf, HC)].astype(F32) * got_pre).astype(BF)

    loop(0, rows // EB, gate_out_other)

    most = pl.ds(0, DP - 1)
    share_desc = remote(gfin.at[most], gfin.at[most], s_rs.at[8], r_rs.at[8], (pair, k))
    share_desc.wait_recv()
    for j in range(DP):
        xx, hh = j // 2, j % 2
        gwt[xx, :, hh * HC:(hh + 1) * HC] = gfin[j].astype(F32)

    for copy in (c_g, c_tok, c_gt, c_pg, c_xr, c_xl, c_xr2, c_xl2):
        copy.wait_send()
    for copy in (c_r1, c_l1, c_r2, c_l2, c_r3, c_l3):
        copy.wait_send()
    remote(wb.at[zs, y, x], wb.at[zs, y, x], s_ag.at[0], r_ag.at[0], (pair, k)).wait_send()
    ag_y_desc.wait_send()
    rs_y_desc.wait_send()
    rs_z_desc.wait_send()
    share_desc.wait_send()
    for ph in range(4):
        for c in range(NC):
            a2a_desc(ph, c).wait_send()


def per_device(Y, CTX, tokens, weight, gate, skip, first, second, kern, third, fourth, cotangent):
    _, rows, D = tokens.shape
    HC = D // 2
    CW = HC // NC
    Z = CTX // Y
    M = 2 * rows
    CH = M // CTX
    R = first.shape[1]
    SL, Q = second.shape[0], second.shape[1]
    WR = D // CTX // X
    vm = pl.BlockSpec(memory_space=pltpu.VMEM)
    out = pl.pallas_call(
        functools.partial(kernel, Y),
        out_shape=(
            jax.ShapeDtypeStruct((rows, D), BF),
            jax.ShapeDtypeStruct((rows, D), BF),
            jax.ShapeDtypeStruct((rows, D), BF),
            jax.ShapeDtypeStruct((X, WR, D), F32),
        ),
        in_specs=[vm] * 10,
        out_specs=(vm,) * 4,
        scratch_shapes=[
            pltpu.VMEM((rows, D), BF),
            pltpu.VMEM((2, rows, HC), BF),
            pltpu.VMEM((rows, HC), BF),
            pltpu.VMEM((2, rows, HC), BF),
            pltpu.VMEM((2, rows, HC), BF),
            pltpu.VMEM((Z, Y, X, WR, HC), BF),
            pltpu.VMEM((Z, Y, X, WR, HC), BF),
            pltpu.VMEM((4, NC, CTX, CH, CW), BF),
            pltpu.VMEM((4, NC, CTX, CH, CW), BF),
            pltpu.VMEM((2, Z // 2, Y, WR, HC), BF),
            pltpu.VMEM((2, Z, Y, WR, HC), BF),
            pltpu.VMEM((Z, Y, WR, HC), BF),
            pltpu.VMEM((Y - 1, Z, WR, HC), BF),
            pltpu.VMEM((Z, WR, HC), BF),
            pltpu.VMEM((Z - 1, WR, HC), BF),
            pltpu.VMEM((WR, HC), BF),
            pltpu.VMEM((2 * X, WR, HC), BF),
            pltpu.VMEM((M, M), BF),
            pltpu.VMEM((M, M), BF),
            pltpu.VMEM((M, M), BF),
            pltpu.VMEM((M, M), BF),
            pltpu.VMEM((SL * Q, M), BF),
            pltpu.VMEM((rows, D), BF),
            pltpu.VMEM((rows, D), BF),
            pltpu.VMEM((rows, HC), BF),
            pltpu.VMEM((rows, HC), BF),
            pltpu.VMEM((2, rows, HC), BF),
            pltpu.SemaphoreType.DMA((6,)),
            pltpu.SemaphoreType.DMA((6,)),
            pltpu.SemaphoreType.DMA((4,)),
            pltpu.SemaphoreType.DMA((4,)),
            pltpu.SemaphoreType.DMA((4, NC)),
            pltpu.SemaphoreType.DMA((4, NC)),
            pltpu.SemaphoreType.DMA((9,)),
            pltpu.SemaphoreType.DMA((9,)),
        ],
        compiler_params=pltpu.CompilerParams(
            collective_id=0, has_side_effects=True, vmem_limit_bytes=60 * 1024 * 1024
        ),
        cost_estimate=pl.CostEstimate(
            flops=8 * rows * D * D, bytes_accessed=8 * rows * D * 2, transcendentals=0
        ),
    )(
        tokens[0],
        weight.reshape(X, WR, D),
        gate[0],
        skip.reshape(1, D),
        first,
        second,
        kern.reshape(Q * SL, D),
        third,
        fourth,
        cotangent[0],
    )
    mixed, gtok, ggate, gwt = out
    return mixed[None], gtok[None], ggate[None], gwt.reshape(X * WR, D)


def solution(mesh, y_size=4):
    in_specs = (
        P("dp", "context", None),
        P("context", None),
        P("dp", "context", None),
        P(),
        P("context", None, None),
        P("context", None, None),
        P(None, "context", None),
        P("context", None, None),
        P("context", None, None),
        P("dp", "context", None),
    )
    out_specs = (
        P("dp", "context", None),
        P("dp", "context", None),
        P("dp", "context", None),
        P("context", None),
    )
    return jax.shard_map(
        functools.partial(per_device, y_size, mesh.shape["context"]),
        mesh=mesh, in_specs=in_specs, out_specs=out_specs, check_vma=False,
    )
```

```python
import functools

import jax
import jax.numpy as jnp
from jax import lax
from jax.experimental import pallas as pl
from jax.experimental.pallas import tpu as pltpu
from jax.sharding import PartitionSpec as P

BF = jnp.bfloat16
F32 = jnp.float32
MESH = pl.DeviceIdType.MESH
X = 4
NC = 2


def mm(a, b):
    return jnp.dot(a, b, preferred_element_type=F32)


def mm_ta(a, b):
    return lax.dot_general(a, b, (((0,), (0,)), ((), ())), preferred_element_type=F32)


def mm_tb(a, b):
    return lax.dot_general(a, b, (((1,), (1,)), ((), ())), preferred_element_type=F32)


def iota(shape, dim):
    return lax.broadcasted_iota(jnp.int32, shape, dim)


def ones_where(cond):
    return jnp.where(cond, 1.0, 0.0).astype(BF)


def loop(lo, hi, body):
    lax.fori_loop(lo, hi, lambda i, c: (body(i), c)[1], 0)


def kernel(
    Y,
    tok, wgt, gate, skip, f1, f2, kern, f3, f4, cot,
    pre, gtown, gtr, gfin,
    tk, tother, gv, cv, kv, g, gx, gp, p, wb, gw, sb, rb, rxa, rxc, sx, ry, sy, rz, fin,
    a1, a2, a3t, a4t, u, gts, gto, pgo,
    s_ag, r_ag, s_pair, r_pair, s_a2a, r_a2a, s_rs, r_rs, s_loc,
):
    dp = lax.axis_index("dp")
    k = lax.axis_index("context")
    DP = 2 * X
    Z = wb.shape[1]
    CTX = Z * Y
    h, x = lax.rem(dp, 2), lax.div(dp, 2)
    z, y = lax.div(k, Y), lax.rem(k, Y)
    right, left = lax.rem(x + 1, X), lax.rem(x + X - 1, X)
    opp = lax.rem(x + 2, X)
    other = 1 - h
    pair = x * 2 + other
    rows, D = tok.shape
    HC = D // 2
    QL, R = f1.shape[0], f1.shape[1]
    SL, Q = f2.shape[0], f2.shape[1]
    M = 2 * rows
    CH = M // CTX
    CW = HC // NC
    WR = wb.shape[4]
    half = pl.multiple_of(h * HC, HC)
    ohalf = pl.multiple_of(other * HC, HC)
    ZH = Z // 2
    TI = D // Z
    rdev, ldev, pdev = (right * 2 + h, k), (left * 2 + h, k), (pair, k)

    def remote(src, dst, ss, rs, dev):
        return pltpu.make_async_remote_copy(
            src_ref=src, dst_ref=dst, send_sem=ss, recv_sem=rs, device_id=dev, device_id_type=MESH
        )

    def local(src, dst, i):
        return pltpu.make_async_copy(src, dst, s_loc.at[i])

    def mine(c):
        return pl.ds(pl.multiple_of(h * HC + c * CW, CW), CW)

    def others(c):
        return pl.ds(pl.multiple_of(other * HC + c * CW, CW), CW)

    in_gate, in_cot = local(gate, gv, 0), local(cot, cv, 1)
    in_kern = local(kern.at[:, :, pl.ds(half, HC)], kv, 2)
    in_tok = local(tok, tk, 3)
    in_w = [local(wgt.at[x, :, mine(c)], wb.at[c, z, y, x], 4 + c) for c in range(NC)]
    in_gate.start()
    in_cot.start()

    barrier = pltpu.get_barrier_semaphore()

    def greet_context(d):
        pl.semaphore_signal(barrier, inc=1, device_id=(dp, lax.rem(k + d, CTX)), device_id_type=MESH)

    def greet_dp(d):
        pl.semaphore_signal(barrier, inc=1, device_id=(lax.rem(dp + d, DP), k), device_id_type=MESH)

    loop(1, DP, greet_dp)
    loop(1, CTX, greet_context)
    for copy in in_w:
        copy.start()
    in_kern.start()
    in_tok.start()

    EB = 32
    in_gate.wait()
    in_cot.wait()

    def gate_rows(i):
        r = pl.ds(pl.multiple_of(i * EB, EB), EB)
        for c in range(NC):
            g[c, h, r, :] = (cv[r, mine(c)].astype(F32) * gv[r, mine(c)].astype(F32)).astype(BF)
            gx[c, r, :] = (cv[r, others(c)].astype(F32) * gv[r, others(c)].astype(F32)).astype(BF)

    loop(0, rows // EB, gate_rows)
    pl.semaphore_wait(barrier, CTX - 1 + DP - 1)

    c_g = [remote(gx.at[c], g.at[c, h], s_pair.at[c], r_pair.at[c], pdev) for c in range(NC)]
    for copy in c_g:
        copy.start()

    def ag_z(c):
        def send(d):
            zz = lax.rem(z + d, Z)
            remote(
                wgt.at[x, :, mine(c)], wb.at[c, z, y, x], s_ag.at[0, c], r_ag.at[0, c], (dp, zz * Y + y)
            ).start()

        loop(1, Z, send)

    def ag_z_desc(c):
        zs = pl.ds(0, Z - 1)
        return remote(wb.at[c, zs, y, x], wb.at[c, zs, y, x], s_ag.at[0, c], r_ag.at[0, c], pdev)

    for c in range(NC):
        ag_z(c)

    def row_matrix(dst, factor, transposed):
        rr, ss = iota((M, R), 0), iota((M, R), 1)
        for b in range(2):
            for q in range(QL):
                e = ones_where(rr == (ss // SL) * CH + b * (QL * SL) + q * SL + ss % SL)
                block = mm_tb(e, factor[q]) if transposed else mm(e, factor[q])
                dst[:, (b * QL + q) * R:(b * QL + q + 1) * R] = block.astype(BF)

    def column_matrix(dst, factor, transposed):
        qq, cc = iota((Q, M), 0), iota((Q, M), 1)
        for s in range(SL):
            e = ones_where(
                (cc // CH == qq // QL) & ((cc // SL) % QL == qq % QL) & (cc % SL == s)
            )
            block = mm_ta(factor[s], e) if transposed else mm(factor[s], e)
            u[s * Q:(s + 1) * Q, :] = block.astype(BF)
        rr, cc = iota((Q * SL, SL * Q), 0), iota((Q * SL, SL * Q), 1)
        move = ones_where((rr // SL == cc % Q) & (rr % SL == cc // Q))
        full = mm(move, u[...])
        owner = (iota((Q * SL, M), 1) // (QL * SL)) % 2
        for b in range(2):
            dst[b * Q * SL:(b + 1) * Q * SL, :] = jnp.where(owner == b, full, 0.0).astype(BF)

    def a2a_start(ph, c):
        def send(d):
            kk = lax.rem(k + d, CTX)
            remote(
                sb.at[ph, c, kk], rb.at[ph, c, k], s_a2a.at[ph, c], r_a2a.at[ph, c], (dp, kk)
            ).start()

        loop(1, CTX, send)
        rb[ph, c, k] = sb[ph, c, k]

    def a2a_desc(ph, c):
        most = pl.ds(0, CTX - 1)
        return remote(
            sb.at[ph, c, most], rb.at[ph, c, most], s_a2a.at[ph, c], r_a2a.at[ph, c],
            (dp, lax.rem(k + 1, CTX)),
        )

    def put(ph, c, value):
        sb[ph, c] = value.astype(BF).reshape(CTX, CH, CW)

    def got(ph, c):
        return rb[ph, c].reshape(M, CW)

    def cols(c):
        return slice(c * CW, (c + 1) * CW)

    row_matrix(a4t, f4, True)

    for c in range(NC):
        c_g[c].wait_recv()
        put(0, c, mm(a4t[...], g[c].reshape(M, CW)))
        a2a_start(0, c)

    def ag_y(c):
        ag_z_desc(c).wait_recv()
        in_w[c].wait()

        def send(d):
            yy = lax.rem(y + d, Y)
            remote(
                wb.at[c, :, y, x], wb.at[c, :, y, x], s_ag.at[1, c], r_ag.at[1, c], (dp, z * Y + yy)
            ).start()

        loop(1, Y, send)

    def ag_y_desc(c):
        ys = pl.ds(0, Y - 1)
        return remote(wb.at[c, :, ys, x], wb.at[c, :, ys, x], s_ag.at[1, c], r_ag.at[1, c], pdev)

    for c in range(NC):
        ag_y(c)
    c_tok = remote(tok, tother, s_pair.at[NC], r_pair.at[NC], pdev)
    c_tok.start()
    column_matrix(a3t, f3, True)

    lo, hi = pl.ds(0, ZH), pl.ds(ZH, Z - ZH)
    c_xr = [remote(wb.at[c, :, :, x], wb.at[c, :, :, x], s_ag.at[2, c], r_ag.at[2, c], rdev) for c in range(NC)]
    c_xl = [remote(wb.at[c, :, :, x], wb.at[c, :, :, x], s_ag.at[3, c], r_ag.at[3, c], ldev) for c in range(NC)]
    c_xr2 = [remote(wb.at[c, lo, :, left], wb.at[c, lo, :, left], s_ag.at[4, c], r_ag.at[4, c], rdev) for c in range(NC)]
    c_xl2 = [remote(wb.at[c, hi, :, right], wb.at[c, hi, :, right], s_ag.at[5, c], r_ag.at[5, c], ldev) for c in range(NC)]

    def ag_x1(c):
        ag_y_desc(c).wait_recv()
        c_xr[c].start()
        c_xl[c].start()

    def ag_x2(c):
        c_xr[c].wait_recv()
        c_xr2[c].start()
        c_xl[c].wait_recv()
        c_xl2[c].start()

    ag_x1(0)
    column_matrix(a2, f2, False)
    for c in range(1, NC):
        ag_x1(c)
    row_matrix(a1, f1, False)

    def filtered(value, c):
        kc = kv[:, :, cols(c)].astype(F32).reshape(Q * SL, CW)
        return (value.reshape(2, Q * SL, CW) * kc[None]).astype(BF).reshape(M, CW)

    def back_columns(c):
        a2a_desc(0, c).wait_recv()
        gs = filtered(mm(a3t[...], got(0, c)), c)
        put(1, c, mm_ta(a2[...], gs))
        a2a_start(1, c)

    def forward_columns(c):
        a2a_desc(2, c).wait_recv()
        fl = filtered(mm(a2[...], got(2, c)), c)
        put(3, c, mm_ta(a3t[...], fl))
        a2a_start(3, c)

    def project(c):
        c_xr2[c].wait_recv()
        c_xl2[c].wait_recv()
        wc = wb[c].reshape(D, CW)
        p[c, h] = mm(tk[...], wc).astype(BF)
        p[c, other] = mm(tother[...], wc).astype(BF)
        put(2, c, mm(a1[...], p[c].reshape(M, CW)))

    def gradient_rows(c):
        gf = mm_ta(a1[...], got(1, c)) + skip[:, mine(c)] * g[c].reshape(M, CW).astype(F32)
        gp[c] = gf.astype(BF).reshape(2, rows, CW)

    def rs_copies(c):
        return (
            remote(gw.at[c, lo, :, opp], rxa.at[c, 0], s_rs.at[0, c], r_rs.at[0, c], rdev),
            remote(gw.at[c, hi, :, opp], rxa.at[c, 1], s_rs.at[1, c], r_rs.at[1, c], ldev),
            remote(gw.at[c, hi, :, right], rxc.at[c, 0, hi], s_rs.at[2, c], r_rs.at[2, c], rdev),
            remote(gw.at[c, lo, :, left], rxc.at[c, 1, lo], s_rs.at[3, c], r_rs.at[3, c], ldev),
            remote(gw.at[c, lo, :, right], rxc.at[c, 0, lo], s_rs.at[4, c], r_rs.at[4, c], rdev),
            remote(gw.at[c, hi, :, left], rxc.at[c, 1, hi], s_rs.at[5, c], r_rs.at[5, c], ldev),
        )

    def rs_x1(c):
        def part_rows(i):
            at = pl.ds(pl.multiple_of(i * TI, TI), TI)
            part = mm_ta(tk[:, at], gp[c, h]) + mm_ta(tother[:, at], gp[c, other])
            gw[c, i] = part.astype(BF).reshape(Y, X, WR, CW)

        loop(0, Z, part_rows)
        for copy in rs_copies(c)[:4]:
            copy.start()

    def rs_x2(c):
        copies = rs_copies(c)

        def add_right(i):
            gw[c, i, :, right] = (gw[c, i, :, right].astype(F32) + rxa[c, 0, i].astype(F32)).astype(BF)

        def add_left(i):
            gw[c, ZH + i, :, left] = (
                gw[c, ZH + i, :, left].astype(F32) + rxa[c, 1, i].astype(F32)
            ).astype(BF)

        copies[0].wait_recv()
        loop(0, ZH, add_right)
        copies[4].start()
        copies[1].wait_recv()
        loop(0, ZH, add_left)
        copies[5].start()

    def rs_y(c):
        for copy in rs_copies(c)[2:]:
            copy.wait_recv()

        def sum_x(i):
            sx[c, i] = (
                gw[c, i, :, x].astype(F32) + rxc[c, 0, i].astype(F32) + rxc[c, 1, i].astype(F32)
            ).astype(BF)

        loop(0, Z, sum_x)

        def send(d):
            yy = lax.rem(y + d, Y)
            remote(
                sx.at[c, :, yy], ry.at[c, d - 1], s_rs.at[6, c], r_rs.at[6, c], (dp, z * Y + yy)
            ).start()

        loop(1, Y, send)

    def rs_y_desc(c):
        return remote(ry.at[c], ry.at[c], s_rs.at[6, c], r_rs.at[6, c], pdev)

    def rs_z(c):
        rs_y_desc(c).wait_recv()

        def sum_y(i):
            total = sx[c, i, y].astype(F32)
            for d in range(Y - 1):
                total = total + ry[c, d, i].astype(F32)
            sy[c, i] = total.astype(BF)

        loop(0, Z, sum_y)

        def send(d):
            zz = lax.rem(z + d, Z)
            remote(
                sy.at[c, zz], rz.at[c, d - 1], s_rs.at[7, c], r_rs.at[7, c], (dp, zz * Y + y)
            ).start()

        loop(1, Z, send)

    def rs_z_desc(c):
        return remote(rz.at[c], rz.at[c], s_rs.at[7, c], r_rs.at[7, c], pdev)

    def rs_sum(c):
        rs_z_desc(c).wait_recv()
        total = sy[c, z].astype(F32)
        for d in range(Z - 1):
            total = total + rz[c, d].astype(F32)
        fin[:, cols(c)] = total.astype(BF)

    def field_rows(c):
        a2a_desc(3, c).wait_recv()
        front = mm_ta(a4t[...], got(3, c)) + skip[:, mine(c)] * p[c].reshape(M, CW).astype(F32)
        pgo[c] = front.astype(BF).reshape(2, rows, CW)

    out_pre = [local(pgo.at[c, h], pre.at[:, mine(c)], 4 + NC + c) for c in range(NC)]
    c_pre = [
        remote(pgo.at[c, other], pre.at[:, mine(c)], s_pair.at[NC + 2 + c], r_pair.at[NC + 2 + c], pdev)
        for c in range(NC)
    ]

    in_kern.wait()
    back_columns(0)
    ag_x2(0)
    for c in range(1, NC):
        back_columns(c)
        ag_x2(c)
    in_tok.wait()
    c_tok.wait_recv()
    project(0)

    a2a_desc(1, 0).wait_recv()
    a2a_start(2, 0)
    gradient_rows(0)
    rs_x1(0)
    for c in range(1, NC):
        project(c)
        rs_x2(c - 1)
        a2a_desc(1, c).wait_recv()
        a2a_start(2, c)
        gradient_rows(c)
        rs_x1(c)

    def token_rows(i, b):
        total = mm_tb(gp[0, b], wb[0, i].reshape(TI, CW))
        for c in range(1, NC):
            total = total + mm_tb(gp[c, b], wb[c, i].reshape(TI, CW))
        return total.astype(BF)

    def gt_other(i):
        gts[:, pl.ds(pl.multiple_of(i * TI, TI), TI)] = token_rows(i, other)

    loop(0, Z, gt_other)
    c_gt = remote(gts, gtr, s_pair.at[NC + 1], r_pair.at[NC + 1], pdev)
    c_gt.start()

    forward_columns(0)
    rs_x2(NC - 1)
    rs_y(0)
    for c in range(1, NC):
        forward_columns(c)
        rs_z(c - 1)
        rs_y(c)

    def gt_own(i):
        gto[:, pl.ds(pl.multiple_of(i * TI, TI), TI)] = token_rows(i, h)

    loop(0, Z, gt_own)
    out_gt = local(gto, gtown, 4 + 2 * NC)
    out_gt.start()

    for c in range(NC - 1):
        rs_sum(c)
        field_rows(c)
        out_pre[c].start()
        c_pre[c].start()
    rs_z(NC - 1)
    rs_sum(NC - 1)
    my_rows = gfin.at[dp]

    def share(d):
        remote(fin, my_rows, s_rs.at[8, 0], r_rs.at[8, 0], (lax.rem(dp + d, DP), k)).start()

    loop(1, DP, share)
    out_fin = local(fin, my_rows, 5 + 2 * NC)
    out_fin.start()
    field_rows(NC - 1)
    out_pre[NC - 1].start()
    c_pre[NC - 1].start()
    share_desc = remote(
        gfin.at[pl.ds(0, DP - 1)], gfin.at[pl.ds(0, DP - 1)], s_rs.at[8, 0], r_rs.at[8, 0], pdev
    )

    for c in range(NC):
        out_pre[c].wait()
        c_pre[c].wait()
        c_g[c].wait_send()
        for copy in (c_xr[c], c_xl[c], c_xr2[c], c_xl2[c], ag_z_desc(c), ag_y_desc(c)):
            copy.wait_send()
        for copy in rs_copies(c):
            copy.wait_send()
        rs_y_desc(c).wait_send()
        rs_z_desc(c).wait_send()
        for ph in range(4):
            a2a_desc(ph, c).wait_send()
    c_tok.wait_send()
    c_gt.wait()
    out_gt.wait()
    out_fin.wait()
    share_desc.wait()


def finish(pre, gate, cot, gtown, gtr, gfin, mixed, gtok, ggate, gwt):
    front = pre[...].astype(F32)
    mixed[...] = (gate[...].astype(F32) * front).astype(BF)
    ggate[...] = (cot[...].astype(F32) * front).astype(BF)
    gtok[...] = (gtown[...].astype(F32) + gtr[...].astype(F32)).astype(BF)
    HC = gfin.shape[2]
    for j in range(2):
        gwt[0, :, j * HC:(j + 1) * HC] = gfin[j].astype(F32)


def per_device(Y, CTX, tokens, weight, gate, skip, first, second, kern, third, fourth, cotangent):
    _, rows, D = tokens.shape
    HC = D // 2
    CW = HC // NC
    Z = CTX // Y
    M = 2 * rows
    CH = M // CTX
    R = first.shape[1]
    SL, Q = second.shape[0], second.shape[1]
    WR = D // CTX // X
    vm = pl.BlockSpec(memory_space=pltpu.VMEM)
    hbm = pl.BlockSpec(memory_space=pl.ANY)
    pre, gtown, gtr, gfin = pl.pallas_call(
        functools.partial(kernel, Y),
        out_shape=(
            jax.ShapeDtypeStruct((rows, D), BF),
            jax.ShapeDtypeStruct((rows, D), BF),
            jax.ShapeDtypeStruct((rows, D), BF),
            jax.ShapeDtypeStruct((2 * X, WR, HC), BF),
        ),
        in_specs=[hbm, hbm, hbm, vm, vm, vm, hbm, vm, vm, hbm],
        out_specs=(hbm,) * 4,
        scratch_shapes=[
            pltpu.VMEM((rows, D), BF),
            pltpu.VMEM((rows, D), BF),
            pltpu.VMEM((rows, D), BF),
            pltpu.VMEM((rows, D), BF),
            pltpu.VMEM((Q, SL, HC), BF),
            pltpu.VMEM((NC, 2, rows, CW), BF),
            pltpu.VMEM((NC, rows, CW), BF),
            pltpu.VMEM((NC, 2, rows, CW), BF),
            pltpu.VMEM((NC, 2, rows, CW), BF),
            pltpu.VMEM((NC, Z, Y, X, WR, CW), BF),
            pltpu.VMEM((NC, Z, Y, X, WR, CW), BF),
            pltpu.VMEM((4, NC, CTX, CH, CW), BF),
            pltpu.VMEM((4, NC, CTX, CH, CW), BF),
            pltpu.VMEM((NC, 2, Z // 2, Y, WR, CW), BF),
            pltpu.VMEM((NC, 2, Z, Y, WR, CW), BF),
            pltpu.VMEM((NC, Z, Y, WR, CW), BF),
            pltpu.VMEM((NC, Y - 1, Z, WR, CW), BF),
            pltpu.VMEM((NC, Z, WR, CW), BF),
            pltpu.VMEM((NC, Z - 1, WR, CW), BF),
            pltpu.VMEM((WR, HC), BF),
            pltpu.VMEM((M, M), BF),
            pltpu.VMEM((M, M), BF),
            pltpu.VMEM((M, M), BF),
            pltpu.VMEM((M, M), BF),
            pltpu.VMEM((SL * Q, M), BF),
            pltpu.VMEM((rows, D), BF),
            pltpu.VMEM((rows, D), BF),
            pltpu.VMEM((NC, 2, rows, CW), BF),
            pltpu.SemaphoreType.DMA((6, NC)),
            pltpu.SemaphoreType.DMA((6, NC)),
            pltpu.SemaphoreType.DMA((2 * NC + 2,)),
            pltpu.SemaphoreType.DMA((2 * NC + 2,)),
            pltpu.SemaphoreType.DMA((4, NC)),
            pltpu.SemaphoreType.DMA((4, NC)),
            pltpu.SemaphoreType.DMA((9, NC)),
            pltpu.SemaphoreType.DMA((9, NC)),
            pltpu.SemaphoreType.DMA((2 * NC + 6,)),
        ],
        compiler_params=pltpu.CompilerParams(
            collective_id=0, has_side_effects=True, vmem_limit_bytes=60 * 1024 * 1024
        ),
        cost_estimate=pl.CostEstimate(
            flops=8 * rows * D * D, bytes_accessed=8 * rows * D * 2, transcendentals=0
        ),
    )(
        tokens[0],
        weight.reshape(X, WR, D),
        gate[0],
        skip.reshape(1, D),
        first,
        second,
        kern,
        third,
        fourth,
        cotangent[0],
    )
    block = pl.BlockSpec((rows // X, D), lambda i: (i, 0))
    wide = pl.BlockSpec((1, WR, D), lambda i: (i, 0, 0))
    two = pl.BlockSpec((2, WR, HC), lambda i: (i, 0, 0))
    mixed, gtok, ggate, gwt = pl.pallas_call(
        finish,
        grid=(X,),
        out_shape=(
            jax.ShapeDtypeStruct((rows, D), BF),
            jax.ShapeDtypeStruct((rows, D), BF),
            jax.ShapeDtypeStruct((rows, D), BF),
            jax.ShapeDtypeStruct((X, WR, D), F32),
        ),
        in_specs=[block, block, block, block, block, two],
        out_specs=(block, block, block, wide),
        compiler_params=pltpu.CompilerParams(vmem_limit_bytes=16 * 1024 * 1024),
        cost_estimate=pl.CostEstimate(
            flops=8 * rows * D, bytes_accessed=16 * rows * D, transcendentals=0
        ),
    )(pre, gate[0], cotangent[0], gtown, gtr, gfin)
    return mixed[None], gtok[None], ggate[None], gwt.reshape(X * WR, D)


def solution(mesh, y_size=4):
    in_specs = (
        P("dp", "context", None),
        P("context", None),
        P("dp", "context", None),
        P(),
        P("context", None, None),
        P("context", None, None),
        P(None, "context", None),
        P("context", None, None),
        P("context", None, None),
        P("dp", "context", None),
    )
    out_specs = (
        P("dp", "context", None),
        P("dp", "context", None),
        P("dp", "context", None),
        P("context", None),
    )
    return jax.shard_map(
        functools.partial(per_device, y_size, mesh.shape["context"]),
        mesh=mesh, in_specs=in_specs, out_specs=out_specs, check_vma=False,
    )
```

```python
import functools

import jax
import jax.numpy as jnp
from jax import lax
from jax.experimental import pallas as pl
from jax.experimental.pallas import tpu as pltpu
from jax.sharding import PartitionSpec as P

BF = jnp.bfloat16
F32 = jnp.float32
MESH = pl.DeviceIdType.MESH
X = 4
NC = 2


def mm(a, b):
    return jnp.dot(a, b, preferred_element_type=F32)


def mm_ta(a, b):
    return lax.dot_general(a, b, (((0,), (0,)), ((), ())), preferred_element_type=F32)


def mm_tb(a, b):
    return lax.dot_general(a, b, (((1,), (1,)), ((), ())), preferred_element_type=F32)


def iota(shape, dim):
    return lax.broadcasted_iota(jnp.int32, shape, dim)


def ones_where(cond):
    return jnp.where(cond, 1.0, 0.0).astype(BF)


def loop(lo, hi, body):
    lax.fori_loop(lo, hi, lambda i, c: (body(i), c)[1], 0)


def kernel(
    Y,
    tok, wgt, gate, skip, f1, f2, kern, f3, f4, cot,
    pre, gtown, gtr, gfin,
    tk, tother, gv, cv, kv, g, gx, gp, p, wb, gw, sb, rb, rxa, rxc, sx, ry, sy, rz, fin,
    a1, a2, a3t, a4t, u, gts, gto, pgo,
    s_ag, r_ag, s_pair, r_pair, s_a2a, r_a2a, s_rs, r_rs, s_loc,
):
    dp = lax.axis_index("dp")
    k = lax.axis_index("context")
    DP = 2 * X
    Z = wb.shape[1]
    CTX = Z * Y
    h, x = lax.rem(dp, 2), lax.div(dp, 2)
    z, y = lax.div(k, Y), lax.rem(k, Y)
    right, left = lax.rem(x + 1, X), lax.rem(x + X - 1, X)
    opp = lax.rem(x + 2, X)
    other = 1 - h
    pair = x * 2 + other
    rows, D = tok.shape
    HC = D // 2
    QL, R = f1.shape[0], f1.shape[1]
    SL, Q = f2.shape[0], f2.shape[1]
    M = 2 * rows
    CH = M // CTX
    CW = HC // NC
    WR = wb.shape[4]
    half = pl.multiple_of(h * HC, HC)
    ohalf = pl.multiple_of(other * HC, HC)
    ZH = Z // 2
    TI = D // Z
    rdev, ldev, pdev = (right * 2 + h, k), (left * 2 + h, k), (pair, k)

    def remote(src, dst, ss, rs, dev):
        return pltpu.make_async_remote_copy(
            src_ref=src, dst_ref=dst, send_sem=ss, recv_sem=rs, device_id=dev, device_id_type=MESH
        )

    def local(src, dst, i):
        return pltpu.make_async_copy(src, dst, s_loc.at[i])

    def mine(c):
        return pl.ds(pl.multiple_of(h * HC + c * CW, CW), CW)

    def others(c):
        return pl.ds(pl.multiple_of(other * HC + c * CW, CW), CW)

    in_gate, in_cot = local(gate, gv, 0), local(cot, cv, 1)
    in_kern = local(kern.at[:, :, pl.ds(half, HC)], kv, 2)
    in_tok = local(tok, tk, 3)
    in_w = [local(wgt.at[x, :, mine(c)], wb.at[c, z, y, x], 4 + c) for c in range(NC)]
    in_gate.start()
    in_cot.start()

    barrier = pltpu.get_barrier_semaphore()

    def greet_context(d):
        pl.semaphore_signal(barrier, inc=1, device_id=(dp, lax.rem(k + d, CTX)), device_id_type=MESH)

    def greet_dp(d):
        pl.semaphore_signal(barrier, inc=1, device_id=(lax.rem(dp + d, DP), k), device_id_type=MESH)

    loop(1, DP, greet_dp)
    loop(1, CTX, greet_context)
    for copy in in_w:
        copy.start()
    in_kern.start()
    in_tok.start()

    EB = 32
    in_gate.wait()
    in_cot.wait()

    def gate_rows(i):
        r = pl.ds(pl.multiple_of(i * EB, EB), EB)
        for c in range(NC):
            g[c, h, r, :] = (cv[r, mine(c)].astype(F32) * gv[r, mine(c)].astype(F32)).astype(BF)
            gx[c, r, :] = (cv[r, others(c)].astype(F32) * gv[r, others(c)].astype(F32)).astype(BF)

    loop(0, rows // EB, gate_rows)
    pl.semaphore_wait(barrier, CTX - 1 + DP - 1)

    c_g = [remote(gx.at[c], g.at[c, h], s_pair.at[c], r_pair.at[c], pdev) for c in range(NC)]
    for copy in c_g:
        copy.start()

    def ag_z(c):
        def send(d):
            zz = lax.rem(z + d, Z)
            remote(
                wgt.at[x, :, mine(c)], wb.at[c, z, y, x], s_ag.at[0, c], r_ag.at[0, c], (dp, zz * Y + y)
            ).start()

        loop(1, Z, send)

    def ag_z_desc(c):
        zs = pl.ds(0, Z - 1)
        return remote(wb.at[c, zs, y, x], wb.at[c, zs, y, x], s_ag.at[0, c], r_ag.at[0, c], pdev)

    for c in range(NC):
        ag_z(c)

    def row_matrix(dst, factor, transposed):
        rr, ss = iota((M, R), 0), iota((M, R), 1)
        for b in range(2):
            for q in range(QL):
                e = ones_where(rr == (ss // SL) * CH + b * (QL * SL) + q * SL + ss % SL)
                block = mm_tb(e, factor[q]) if transposed else mm(e, factor[q])
                dst[:, (b * QL + q) * R:(b * QL + q + 1) * R] = block.astype(BF)

    def column_matrix(dst, factor, transposed):
        qq, cc = iota((Q, M), 0), iota((Q, M), 1)
        for s in range(SL):
            e = ones_where(
                (cc // CH == qq // QL) & ((cc // SL) % QL == qq % QL) & (cc % SL == s)
            )
            block = mm_ta(factor[s], e) if transposed else mm(factor[s], e)
            u[s * Q:(s + 1) * Q, :] = block.astype(BF)
        rr, cc = iota((Q * SL, SL * Q), 0), iota((Q * SL, SL * Q), 1)
        move = ones_where((rr // SL == cc % Q) & (rr % SL == cc // Q))
        full = mm(move, u[...])
        owner = (iota((Q * SL, M), 1) // (QL * SL)) % 2
        for b in range(2):
            dst[b * Q * SL:(b + 1) * Q * SL, :] = jnp.where(owner == b, full, 0.0).astype(BF)

    def a2a_send(ph, c, lo, hi, step):
        def send(i):
            kk = lax.rem(k + i * step + 1, CTX)
            remote(
                sb.at[ph, c, kk], rb.at[ph, c, k], s_a2a.at[ph, c], r_a2a.at[ph, c], (dp, kk)
            ).start()

        loop(lo, hi, send)

    def a2a_start(ph, c):
        a2a_send(ph, c, 0, CTX - 1, 1)
        rb[ph, c, k] = sb[ph, c, k]

    def a2a_start_odd(ph, c):
        a2a_send(ph, c, 0, CTX // 2, 2)
        rb[ph, c, k] = sb[ph, c, k]

    def a2a_start_even(ph, c):
        def send(i):
            kk = lax.rem(k + 2 * i, CTX)
            remote(
                sb.at[ph, c, kk], rb.at[ph, c, k], s_a2a.at[ph, c], r_a2a.at[ph, c], (dp, kk)
            ).start()

        loop(1, CTX // 2, send)

    def a2a_desc(ph, c):
        most = pl.ds(0, CTX - 1)
        return remote(
            sb.at[ph, c, most], rb.at[ph, c, most], s_a2a.at[ph, c], r_a2a.at[ph, c],
            (dp, lax.rem(k + 1, CTX)),
        )

    def put(ph, c, value):
        sb[ph, c] = value.astype(BF).reshape(CTX, CH, CW)

    def got(ph, c):
        return rb[ph, c].reshape(M, CW)

    def cols(c):
        return slice(c * CW, (c + 1) * CW)

    row_matrix(a4t, f4, True)

    def ag_y(c):
        ag_z_desc(c).wait_recv()
        in_w[c].wait()

        def send(d):
            yy = lax.rem(y + d, Y)
            remote(
                wb.at[c, :, y, x], wb.at[c, :, y, x], s_ag.at[1, c], r_ag.at[1, c], (dp, z * Y + yy)
            ).start()

        loop(1, Y, send)

    def ag_y_desc(c):
        ys = pl.ds(0, Y - 1)
        return remote(wb.at[c, :, ys, x], wb.at[c, :, ys, x], s_ag.at[1, c], r_ag.at[1, c], pdev)

    for c in range(NC):
        c_g[c].wait_recv()
        put(0, c, mm(a4t[...], g[c].reshape(M, CW)))
        a2a_start(0, c)
        ag_y(c)
    c_tok = remote(tok, tother, s_pair.at[NC], r_pair.at[NC], pdev)
    c_tok.start()
    column_matrix(a3t, f3, True)

    lo, hi = pl.ds(0, ZH), pl.ds(ZH, Z - ZH)
    c_xr = [remote(wb.at[c, :, :, x], wb.at[c, :, :, x], s_ag.at[2, c], r_ag.at[2, c], rdev) for c in range(NC)]
    c_xl = [remote(wb.at[c, :, :, x], wb.at[c, :, :, x], s_ag.at[3, c], r_ag.at[3, c], ldev) for c in range(NC)]
    c_xr2 = [remote(wb.at[c, lo, :, left], wb.at[c, lo, :, left], s_ag.at[4, c], r_ag.at[4, c], rdev) for c in range(NC)]
    c_xl2 = [remote(wb.at[c, hi, :, right], wb.at[c, hi, :, right], s_ag.at[5, c], r_ag.at[5, c], ldev) for c in range(NC)]

    def ag_x1(c):
        ag_y_desc(c).wait_recv()
        c_xr[c].start()
        c_xl[c].start()

    def ag_x2(c):
        c_xr[c].wait_recv()
        c_xr2[c].start()
        c_xl[c].wait_recv()
        c_xl2[c].start()

    ag_x1(0)
    column_matrix(a2, f2, False)
    for c in range(1, NC):
        ag_x1(c)
    row_matrix(a1, f1, False)

    def filtered(value, c):
        kc = kv[:, :, cols(c)].astype(F32).reshape(Q * SL, CW)
        return (value.reshape(2, Q * SL, CW) * kc[None]).astype(BF).reshape(M, CW)

    def back_columns(c):
        a2a_desc(0, c).wait_recv()
        gs = filtered(mm(a3t[...], got(0, c)), c)
        put(1, c, mm_ta(a2[...], gs))
        a2a_start(1, c)

    def forward_columns(c):
        a2a_desc(2, c).wait_recv()
        fl = filtered(mm(a2[...], got(2, c)), c)
        put(3, c, mm_ta(a3t[...], fl))
        if c < NC - 1:
            a2a_start(3, c)
        else:
            a2a_start_odd(3, c)

    def project(c):
        c_xr2[c].wait_recv()
        c_xl2[c].wait_recv()
        wc = wb[c].reshape(D, CW)
        p[c, h] = mm(tk[...], wc).astype(BF)
        p[c, other] = mm(tother[...], wc).astype(BF)
        put(2, c, mm(a1[...], p[c].reshape(M, CW)))

    def gradient_rows(c):
        gf = mm_ta(a1[...], got(1, c)) + skip[:, mine(c)] * g[c].reshape(M, CW).astype(F32)
        gp[c] = gf.astype(BF).reshape(2, rows, CW)

    def rs_copies(c):
        return (
            remote(gw.at[c, lo, :, opp], rxa.at[c, 0], s_rs.at[0, c], r_rs.at[0, c], rdev),
            remote(gw.at[c, hi, :, opp], rxa.at[c, 1], s_rs.at[1, c], r_rs.at[1, c], ldev),
            remote(gw.at[c, hi, :, right], rxc.at[c, 0, hi], s_rs.at[2, c], r_rs.at[2, c], rdev),
            remote(gw.at[c, lo, :, left], rxc.at[c, 1, lo], s_rs.at[3, c], r_rs.at[3, c], ldev),
            remote(gw.at[c, lo, :, right], rxc.at[c, 0, lo], s_rs.at[4, c], r_rs.at[4, c], rdev),
            remote(gw.at[c, hi, :, left], rxc.at[c, 1, hi], s_rs.at[5, c], r_rs.at[5, c], ldev),
        )

    def rs_x1(c):
        def part_rows(i):
            at = pl.ds(pl.multiple_of(i * TI, TI), TI)
            part = mm_ta(tk[:, at], gp[c, h]) + mm_ta(tother[:, at], gp[c, other])
            gw[c, i] = part.astype(BF).reshape(Y, X, WR, CW)

        loop(0, Z, part_rows)
        for copy in rs_copies(c)[:4]:
            copy.start()

    def rs_x2(c):
        copies = rs_copies(c)

        def add_right(i):
            gw[c, i, :, right] = (gw[c, i, :, right].astype(F32) + rxa[c, 0, i].astype(F32)).astype(BF)

        def add_left(i):
            gw[c, ZH + i, :, left] = (
                gw[c, ZH + i, :, left].astype(F32) + rxa[c, 1, i].astype(F32)
            ).astype(BF)

        copies[0].wait_recv()
        loop(0, ZH, add_right)
        copies[4].start()
        copies[1].wait_recv()
        loop(0, ZH, add_left)
        copies[5].start()

    def rs_y(c):
        for copy in rs_copies(c)[2:]:
            copy.wait_recv()

        def sum_x(i):
            sx[c, i] = (
                gw[c, i, :, x].astype(F32) + rxc[c, 0, i].astype(F32) + rxc[c, 1, i].astype(F32)
            ).astype(BF)

        loop(0, Z, sum_x)

        def send(d):
            yy = lax.rem(y + d, Y)
            remote(
                sx.at[c, :, yy], ry.at[c, d - 1], s_rs.at[6, c], r_rs.at[6, c], (dp, z * Y + yy)
            ).start()

        loop(1, Y, send)

    def rs_y_desc(c):
        return remote(ry.at[c], ry.at[c], s_rs.at[6, c], r_rs.at[6, c], pdev)

    def rs_z(c):
        rs_y_desc(c).wait_recv()

        def sum_y(i):
            total = sx[c, i, y].astype(F32)
            for d in range(Y - 1):
                total = total + ry[c, d, i].astype(F32)
            sy[c, i] = total.astype(BF)

        loop(0, Z, sum_y)

        def send(d):
            zz = lax.rem(z + d, Z)
            remote(
                sy.at[c, zz], rz.at[c, d - 1], s_rs.at[7, c], r_rs.at[7, c], (dp, zz * Y + y)
            ).start()

        loop(1, Z, send)

    def rs_z_desc(c):
        return remote(rz.at[c], rz.at[c], s_rs.at[7, c], r_rs.at[7, c], pdev)

    def rs_sum(c):
        rs_z_desc(c).wait_recv()
        total = sy[c, z].astype(F32)
        for d in range(Z - 1):
            total = total + rz[c, d].astype(F32)
        fin[:, cols(c)] = total.astype(BF)

    def field_rows(c):
        a2a_desc(3, c).wait_recv()
        front = mm_ta(a4t[...], got(3, c)) + skip[:, mine(c)] * p[c].reshape(M, CW).astype(F32)
        pgo[c] = front.astype(BF).reshape(2, rows, CW)

    out_pre = [local(pgo.at[c, h], pre.at[:, mine(c)], 4 + NC + c) for c in range(NC)]
    c_pre = [
        remote(pgo.at[c, other], pre.at[:, mine(c)], s_pair.at[NC + 2 + c], r_pair.at[NC + 2 + c], pdev)
        for c in range(NC)
    ]

    in_kern.wait()
    back_columns(0)
    ag_x2(0)
    for c in range(1, NC):
        back_columns(c)
        ag_x2(c)
    in_tok.wait()
    c_tok.wait_recv()
    project(0)

    a2a_desc(1, 0).wait_recv()
    a2a_start(2, 0)
    gradient_rows(0)
    rs_x1(0)
    for c in range(1, NC):
        project(c)
        rs_x2(c - 1)
        a2a_desc(1, c).wait_recv()
        a2a_start(2, c)
        gradient_rows(c)
        rs_x1(c)

    def token_rows(i, b):
        total = mm_tb(gp[0, b], wb[0, i].reshape(TI, CW))
        for c in range(1, NC):
            total = total + mm_tb(gp[c, b], wb[c, i].reshape(TI, CW))
        return total.astype(BF)

    def gt_other(i):
        gts[:, pl.ds(pl.multiple_of(i * TI, TI), TI)] = token_rows(i, other)

    loop(0, Z, gt_other)
    c_gt = remote(gts, gtr, s_pair.at[NC + 1], r_pair.at[NC + 1], pdev)
    c_gt.start()

    forward_columns(0)
    rs_x2(NC - 1)
    rs_y(0)
    for c in range(1, NC):
        forward_columns(c)
        rs_z(c - 1)
        rs_y(c)
    a2a_start_even(3, NC - 1)

    def gt_own(i):
        gto[:, pl.ds(pl.multiple_of(i * TI, TI), TI)] = token_rows(i, h)

    loop(0, Z, gt_own)
    out_gt = local(gto, gtown, 4 + 2 * NC)
    out_gt.start()

    for c in range(NC - 1):
        rs_sum(c)
        field_rows(c)
        out_pre[c].start()
        c_pre[c].start()
    rs_z(NC - 1)
    rs_sum(NC - 1)
    my_rows = gfin.at[dp]

    def share(d):
        remote(fin, my_rows, s_rs.at[8, 0], r_rs.at[8, 0], (lax.rem(dp + d, DP), k)).start()

    loop(1, DP, share)
    out_fin = local(fin, my_rows, 5 + 2 * NC)
    out_fin.start()
    field_rows(NC - 1)
    out_pre[NC - 1].start()
    c_pre[NC - 1].start()
    share_desc = remote(
        gfin.at[pl.ds(0, DP - 1)], gfin.at[pl.ds(0, DP - 1)], s_rs.at[8, 0], r_rs.at[8, 0], pdev
    )

    for c in range(NC):
        out_pre[c].wait()
        c_pre[c].wait()
        c_g[c].wait_send()
        for copy in (c_xr[c], c_xl[c], c_xr2[c], c_xl2[c], ag_z_desc(c), ag_y_desc(c)):
            copy.wait_send()
        for copy in rs_copies(c):
            copy.wait_send()
        rs_y_desc(c).wait_send()
        rs_z_desc(c).wait_send()
        for ph in range(4):
            a2a_desc(ph, c).wait_send()
    c_tok.wait_send()
    c_gt.wait()
    out_gt.wait()
    out_fin.wait()
    share_desc.wait()


def finish(pre, gate, cot, gtown, gtr, gfin, mixed, gtok, ggate, gwt):
    front = pre[...].astype(F32)
    mixed[...] = (gate[...].astype(F32) * front).astype(BF)
    ggate[...] = (cot[...].astype(F32) * front).astype(BF)
    gtok[...] = (gtown[...].astype(F32) + gtr[...].astype(F32)).astype(BF)
    HC = gfin.shape[2]
    for j in range(2):
        gwt[0, :, j * HC:(j + 1) * HC] = gfin[j].astype(F32)


def per_device(Y, CTX, tokens, weight, gate, skip, first, second, kern, third, fourth, cotangent):
    _, rows, D = tokens.shape
    HC = D // 2
    CW = HC // NC
    Z = CTX // Y
    M = 2 * rows
    CH = M // CTX
    R = first.shape[1]
    SL, Q = second.shape[0], second.shape[1]
    WR = D // CTX // X
    vm = pl.BlockSpec(memory_space=pltpu.VMEM)
    hbm = pl.BlockSpec(memory_space=pl.ANY)
    pre, gtown, gtr, gfin = pl.pallas_call(
        functools.partial(kernel, Y),
        out_shape=(
            pltpu.VMEM((rows, D), BF),
            pltpu.VMEM((rows, D), BF),
            pltpu.VMEM((rows, D), BF),
            pltpu.VMEM((2 * X, WR, HC), BF),
        ),
        in_specs=[hbm, hbm, hbm, vm, vm, vm, hbm, vm, vm, hbm],
        out_specs=(vm,) * 4,
        scratch_shapes=[
            pltpu.VMEM((rows, D), BF),
            pltpu.VMEM((rows, D), BF),
            pltpu.VMEM((rows, D), BF),
            pltpu.VMEM((rows, D), BF),
            pltpu.VMEM((Q, SL, HC), BF),
            pltpu.VMEM((NC, 2, rows, CW), BF),
            pltpu.VMEM((NC, rows, CW), BF),
            pltpu.VMEM((NC, 2, rows, CW), BF),
            pltpu.VMEM((NC, 2, rows, CW), BF),
            pltpu.VMEM((NC, Z, Y, X, WR, CW), BF),
            pltpu.VMEM((NC, Z, Y, X, WR, CW), BF),
            pltpu.VMEM((4, NC, CTX, CH, CW), BF),
            pltpu.VMEM((4, NC, CTX, CH, CW), BF),
            pltpu.VMEM((NC, 2, Z // 2, Y, WR, CW), BF),
            pltpu.VMEM((NC, 2, Z, Y, WR, CW), BF),
            pltpu.VMEM((NC, Z, Y, WR, CW), BF),
            pltpu.VMEM((NC, Y - 1, Z, WR, CW), BF),
            pltpu.VMEM((NC, Z, WR, CW), BF),
            pltpu.VMEM((NC, Z - 1, WR, CW), BF),
            pltpu.VMEM((WR, HC), BF),
            pltpu.VMEM((M, M), BF),
            pltpu.VMEM((M, M), BF),
            pltpu.VMEM((M, M), BF),
            pltpu.VMEM((M, M), BF),
            pltpu.VMEM((SL * Q, M), BF),
            pltpu.VMEM((rows, D), BF),
            pltpu.VMEM((rows, D), BF),
            pltpu.VMEM((NC, 2, rows, CW), BF),
            pltpu.SemaphoreType.DMA((6, NC)),
            pltpu.SemaphoreType.DMA((6, NC)),
            pltpu.SemaphoreType.DMA((2 * NC + 2,)),
            pltpu.SemaphoreType.DMA((2 * NC + 2,)),
            pltpu.SemaphoreType.DMA((4, NC)),
            pltpu.SemaphoreType.DMA((4, NC)),
            pltpu.SemaphoreType.DMA((9, NC)),
            pltpu.SemaphoreType.DMA((9, NC)),
            pltpu.SemaphoreType.DMA((2 * NC + 6,)),
        ],
        compiler_params=pltpu.CompilerParams(
            collective_id=0, has_side_effects=True, vmem_limit_bytes=52 * 1024 * 1024
        ),
        cost_estimate=pl.CostEstimate(
            flops=8 * rows * D * D, bytes_accessed=8 * rows * D * 2, transcendentals=0
        ),
    )(
        tokens[0],
        weight.reshape(X, WR, D),
        gate[0],
        skip.reshape(1, D),
        first,
        second,
        kern,
        third,
        fourth,
        cotangent[0],
    )
    block = pl.BlockSpec((rows // X, D), lambda i: (i, 0))
    wide = pl.BlockSpec((1, WR, D), lambda i: (i, 0, 0))
    two = pl.BlockSpec((2, WR, HC), lambda i: (i, 0, 0))
    mixed, gtok, ggate, gwt = pl.pallas_call(
        finish,
        grid=(X,),
        out_shape=(
            jax.ShapeDtypeStruct((rows, D), BF),
            jax.ShapeDtypeStruct((rows, D), BF),
            jax.ShapeDtypeStruct((rows, D), BF),
            jax.ShapeDtypeStruct((X, WR, D), F32),
        ),
        in_specs=[block, block, block, block, block, two],
        out_specs=(block, block, block, wide),
        compiler_params=pltpu.CompilerParams(vmem_limit_bytes=16 * 1024 * 1024),
        cost_estimate=pl.CostEstimate(
            flops=8 * rows * D, bytes_accessed=16 * rows * D, transcendentals=0
        ),
    )(pre, gate[0], cotangent[0], gtown, gtr, gfin)
    return mixed[None], gtok[None], ggate[None], gwt.reshape(X * WR, D)


def solution(mesh, y_size=4):
    in_specs = (
        P("dp", "context", None),
        P("context", None),
        P("dp", "context", None),
        P(),
        P("context", None, None),
        P("context", None, None),
        P(None, "context", None),
        P("context", None, None),
        P("context", None, None),
        P("dp", "context", None),
    )
    out_specs = (
        P("dp", "context", None),
        P("dp", "context", None),
        P("dp", "context", None),
        P("context", None),
    )
    return jax.shard_map(
        functools.partial(per_device, y_size, mesh.shape["context"]),
        mesh=mesh, in_specs=in_specs, out_specs=out_specs, check_vma=False,
    )
```

```python
import functools

import jax
import jax.numpy as jnp
from jax import lax
from jax.experimental import pallas as pl
from jax.experimental.pallas import tpu as pltpu
from jax.sharding import PartitionSpec as P

BF = jnp.bfloat16
F32 = jnp.float32
MESH = pl.DeviceIdType.MESH
X = 4
NC = 2


def mm(a, b):
    return jnp.dot(a, b, preferred_element_type=F32)


def mm_ta(a, b):
    return lax.dot_general(a, b, (((0,), (0,)), ((), ())), preferred_element_type=F32)


def mm_tb(a, b):
    return lax.dot_general(a, b, (((1,), (1,)), ((), ())), preferred_element_type=F32)


def iota(shape, dim):
    return lax.broadcasted_iota(jnp.int32, shape, dim)


def ones_where(cond):
    return jnp.where(cond, 1.0, 0.0).astype(BF)


def loop(lo, hi, body):
    lax.fori_loop(lo, hi, lambda i, c: (body(i), c)[1], 0)


def kernel(
    Y,
    tok, wgt, gate, skip_in, f1_in, f2_in, kern, f3_in, f4_in, cot,
    pre, gtown, gtr, gfin,
    f1, f2, f3, f4, skip, a4, tk, tother, gv, cv, kv, g, gx, gp, p, wb, gw, sb, rb, rxa, rxc, sx, ry, sy, rz, fin,
    a1, a2, a3t, a4t, u, gts, gto, pgo,
    s_ag, r_ag, s_pair, r_pair, s_a2a, r_a2a, s_rs, r_rs, s_loc,
):
    dp = lax.axis_index("dp")
    k = lax.axis_index("context")
    DP = 2 * X
    Z = wb.shape[1]
    CTX = Z * Y
    h, x = lax.rem(dp, 2), lax.div(dp, 2)
    z, y = lax.div(k, Y), lax.rem(k, Y)
    right, left = lax.rem(x + 1, X), lax.rem(x + X - 1, X)
    opp = lax.rem(x + 2, X)
    other = 1 - h
    pair = x * 2 + other
    rows, D = tok.shape
    HC = D // 2
    QL, R = f1.shape[0], f1.shape[1]
    SL, Q = f2.shape[0], f2.shape[1]
    M = 2 * rows
    CH = M // CTX
    CW = HC // NC
    WR = wb.shape[4]
    half = pl.multiple_of(h * HC, HC)
    ohalf = pl.multiple_of(other * HC, HC)
    ZH = Z // 2
    TI = D // Z
    rdev, ldev, pdev = (right * 2 + h, k), (left * 2 + h, k), (pair, k)

    def remote(src, dst, ss, rs, dev):
        return pltpu.make_async_remote_copy(
            src_ref=src, dst_ref=dst, send_sem=ss, recv_sem=rs, device_id=dev, device_id_type=MESH
        )

    def local(src, dst, i):
        return pltpu.make_async_copy(src, dst, s_loc.at[i])

    def mine(c):
        return pl.ds(pl.multiple_of(h * HC + c * CW, CW), CW)

    def others(c):
        return pl.ds(pl.multiple_of(other * HC + c * CW, CW), CW)

    in_gate, in_cot = local(gate, gv, 0), local(cot, cv, 1)
    in_kern = local(kern.at[:, :, pl.ds(half, HC)], kv, 2)
    in_tok = local(tok, tk, 3)
    in_w = [local(wgt.at[x, :, mine(c)], wb.at[c, z, y, x], 4 + c) for c in range(NC)]
    small = [
        local(src, dst, 6 + 2 * NC + i)
        for i, (src, dst) in enumerate(
            ((f4_in, f4), (f3_in, f3), (f2_in, f2), (f1_in, f1), (skip_in, skip))
        )
    ]

    barrier = pltpu.get_barrier_semaphore()

    def greet_context(d):
        pl.semaphore_signal(barrier, inc=1, device_id=(dp, lax.rem(k + d, CTX)), device_id_type=MESH)

    def greet_dp(d):
        pl.semaphore_signal(barrier, inc=1, device_id=(lax.rem(dp + d, DP), k), device_id_type=MESH)

    loop(1, CTX, greet_context)
    loop(1, DP, greet_dp)
    in_gate.start()
    in_cot.start()
    for copy in small + in_w:
        copy.start()
    in_kern.start()
    in_tok.start()

    EB = 32
    in_gate.wait()
    in_cot.wait()

    def gate_rows(i):
        r = pl.ds(pl.multiple_of(i * EB, EB), EB)
        for c in range(NC):
            g[c, h, r, :] = (cv[r, mine(c)].astype(F32) * gv[r, mine(c)].astype(F32)).astype(BF)
            gx[c, r, :] = (cv[r, others(c)].astype(F32) * gv[r, others(c)].astype(F32)).astype(BF)

    loop(0, rows // EB, gate_rows)
    pl.semaphore_wait(barrier, CTX - 1 + DP - 1)

    c_g = [remote(gx.at[c], g.at[c, h], s_pair.at[c], r_pair.at[c], pdev) for c in range(NC)]
    for copy in c_g:
        copy.start()

    def ag_z(c):
        def send(d):
            zz = lax.rem(z + d, Z)
            remote(
                wgt.at[x, :, mine(c)], wb.at[c, z, y, x], s_ag.at[0, c], r_ag.at[0, c], (dp, zz * Y + y)
            ).start()

        loop(1, Z, send)

    def ag_z_desc(c):
        zs = pl.ds(0, Z - 1)
        return remote(wb.at[c, zs, y, x], wb.at[c, zs, y, x], s_ag.at[0, c], r_ag.at[0, c], pdev)

    for c in range(NC):
        ag_z(c)

    def row_matrix(dst, factor, transposed):
        rr, ss = iota((M, R), 0), iota((M, R), 1)
        for b in range(2):
            for q in range(QL):
                e = ones_where(rr == (ss // SL) * CH + b * (QL * SL) + q * SL + ss % SL)
                block = mm_tb(e, factor[q]) if transposed else mm(e, factor[q])
                dst[:, (b * QL + q) * R:(b * QL + q + 1) * R] = block.astype(BF)

    def column_matrix(dst, factor, transposed):
        qq, cc = iota((Q, M), 0), iota((Q, M), 1)
        for s in range(SL):
            e = ones_where(
                (cc // CH == qq // QL) & ((cc // SL) % QL == qq % QL) & (cc % SL == s)
            )
            block = mm_ta(factor[s], e) if transposed else mm(factor[s], e)
            u[s * Q:(s + 1) * Q, :] = block.astype(BF)
        rr, cc = iota((Q * SL, SL * Q), 0), iota((Q * SL, SL * Q), 1)
        move = ones_where((rr // SL == cc % Q) & (rr % SL == cc // Q))
        full = mm(move, u[...])
        owner = (iota((Q * SL, M), 1) // (QL * SL)) % 2
        for b in range(2):
            dst[b * Q * SL:(b + 1) * Q * SL, :] = jnp.where(owner == b, full, 0.0).astype(BF)

    def a2a_send(ph, c, lo, hi, step):
        def send(i):
            kk = lax.rem(k + i * step + 1, CTX)
            remote(
                sb.at[ph, c, kk], rb.at[ph, c, k], s_a2a.at[ph, c], r_a2a.at[ph, c], (dp, kk)
            ).start()

        loop(lo, hi, send)

    def a2a_start(ph, c):
        a2a_send(ph, c, 0, CTX - 1, 1)
        rb[ph, c, k] = sb[ph, c, k]

    def a2a_start_odd(ph, c):
        a2a_send(ph, c, 0, CTX // 2, 2)
        rb[ph, c, k] = sb[ph, c, k]

    def a2a_start_even(ph, c):
        def send(i):
            kk = lax.rem(k + 2 * i, CTX)
            remote(
                sb.at[ph, c, kk], rb.at[ph, c, k], s_a2a.at[ph, c], r_a2a.at[ph, c], (dp, kk)
            ).start()

        loop(1, CTX // 2, send)

    def a2a_desc(ph, c):
        most = pl.ds(0, CTX - 1)
        return remote(
            sb.at[ph, c, most], rb.at[ph, c, most], s_a2a.at[ph, c], r_a2a.at[ph, c],
            (dp, lax.rem(k + 1, CTX)),
        )

    def put(ph, c, value):
        sb[ph, c] = value.astype(BF).reshape(CTX, CH, CW)

    def got(ph, c):
        return rb[ph, c].reshape(M, CW)

    def cols(c):
        return slice(c * CW, (c + 1) * CW)

    small[0].wait()
    row_matrix(a4t, f4, True)

    near = sorted(range(1, Y), key=lambda d: min(d, Y - d))

    def ag_y_copy(c, d):
        to = (dp, z * Y + lax.rem(y + d, Y))
        return remote(wb.at[c, :, y, x], wb.at[c, :, y, x], s_ag.at[d, c], r_ag.at[d, c], to)

    def ag_x1_copies(c, d):
        block = wb.at[c, :, lax.rem(y - d + Y, Y), x]
        return (
            remote(block, block, s_ag.at[Y + d, c], r_ag.at[Y + d, c], rdev),
            remote(block, block, s_ag.at[2 * Y + d, c], r_ag.at[2 * Y + d, c], ldev),
        )

    def ag_x1_send(c, d):
        for copy in ag_x1_copies(c, d):
            copy.start()

    def ag_y(c):
        ag_z_desc(c).wait_recv()
        in_w[c].wait()
        for d in near:
            ag_y_copy(c, d).start()
        ag_x1_send(c, 0)

    for c in range(NC):
        c_g[c].wait_recv()
        put(0, c, mm(a4t[...], g[c].reshape(M, CW)))
        a2a_start(0, c)
        ag_y(c)
    c_tok = remote(tok, tother, s_pair.at[NC], r_pair.at[NC], pdev)
    c_tok.start()
    for copy in small[1:]:
        copy.wait()
    column_matrix(a3t, f3, True)

    lo, hi = pl.ds(0, ZH), pl.ds(ZH, Z - ZH)
    last = 3 * Y
    c_xr2 = [
        remote(wb.at[c, lo, :, left], wb.at[c, lo, :, left], s_ag.at[last, c], r_ag.at[last, c], rdev)
        for c in range(NC)
    ]
    c_xl2 = [
        remote(wb.at[c, hi, :, right], wb.at[c, hi, :, right], s_ag.at[last + 1, c], r_ag.at[last + 1, c], ldev)
        for c in range(NC)
    ]

    def ag_x1(c):
        for d in near:
            ag_y_copy(c, d).wait_recv()
            ag_x1_send(c, d)

    def ag_x2(c):
        for d in range(Y):
            ag_x1_copies(c, d)[0].wait_recv()
        c_xr2[c].start()
        for d in range(Y):
            ag_x1_copies(c, d)[1].wait_recv()
        c_xl2[c].start()

    ag_x1(0)
    column_matrix(a2, f2, False)
    for c in range(1, NC):
        ag_x1(c)
    row_matrix(a1, f1, False)
    a4[...] = a4t[...].T

    def filtered(value, c):
        kc = kv[:, :, cols(c)].astype(F32).reshape(Q * SL, CW)
        return (value.reshape(2, Q * SL, CW) * kc[None]).astype(BF).reshape(M, CW)

    def back_columns(c):
        a2a_desc(0, c).wait_recv()
        gs = filtered(mm(a3t[...], got(0, c)), c)
        put(1, c, mm_ta(a2[...], gs))

    def forward_columns(c):
        a2a_desc(2, c).wait_recv()
        fl = filtered(mm(a2[...], got(2, c)), c)
        put(3, c, mm_ta(a3t[...], fl))

    def project(c):
        c_xr2[c].wait_recv()
        c_xl2[c].wait_recv()
        wc = wb[c].reshape(D, CW)
        p[c, h] = mm(tk[...], wc).astype(BF)
        p[c, other] = mm(tother[...], wc).astype(BF)
        put(2, c, mm(a1[...], p[c].reshape(M, CW)))

    def gradient_rows(c):
        gf = mm_ta(a1[...], got(1, c)) + skip[:, mine(c)] * g[c].reshape(M, CW).astype(F32)
        gp[c] = gf.astype(BF).reshape(2, rows, CW)

    def rs_copies(c, own):
        yb = pl.ds(0, 1) if own else pl.ds(1, Y - 1)
        at = 6 if own else 0
        moves = (
            (gw.at[c, lo, yb, opp], rxa.at[c, 0, :, yb], rdev),
            (gw.at[c, hi, yb, opp], rxa.at[c, 1, :, yb], ldev),
            (gw.at[c, hi, yb, right], rxc.at[c, 0, hi, yb], rdev),
            (gw.at[c, lo, yb, left], rxc.at[c, 1, lo, yb], ldev),
            (gw.at[c, lo, yb, right], rxc.at[c, 0, lo, yb], rdev),
            (gw.at[c, hi, yb, left], rxc.at[c, 1, hi, yb], ldev),
        )
        return [
            remote(src, dst, s_rs.at[at + i, c], r_rs.at[at + i, c], dev)
            for i, (src, dst, dev) in enumerate(moves)
        ]

    def rs_x1(c):
        def part_rows(i):
            at = pl.ds(pl.multiple_of(i * TI, TI), TI)
            part = mm_ta(tk[:, at], gp[c, h]) + mm_ta(tother[:, at], gp[c, other])
            part = part.astype(BF).reshape(Y, X, WR, CW)
            for yy in range(Y):
                gw[c, i, lax.rem(yy - y + Y, Y)] = part[yy]

        loop(0, Z, part_rows)
        for copy in rs_copies(c, False)[:4]:
            copy.start()

    def rs_pass(c, own):
        copies = rs_copies(c, own)
        blocks = range(0, 1) if own else range(1, Y)

        def add_right(i):
            for r in blocks:
                gw[c, i, r, right] = (
                    gw[c, i, r, right].astype(F32) + rxa[c, 0, i, r].astype(F32)
                ).astype(BF)

        def add_left(i):
            for r in blocks:
                gw[c, ZH + i, r, left] = (
                    gw[c, ZH + i, r, left].astype(F32) + rxa[c, 1, i, r].astype(F32)
                ).astype(BF)

        copies[0].wait_recv()
        loop(0, ZH, add_right)
        copies[4].start()
        copies[1].wait_recv()
        loop(0, ZH, add_left)
        copies[5].start()

    def rs_x2(c):
        rs_pass(c, False)
        for copy in rs_copies(c, True)[:4]:
            copy.start()

    def rs_x3(c):
        rs_pass(c, True)

    def sum_x(c, own):
        for copy in rs_copies(c, own)[2:]:
            copy.wait_recv()
        blocks = range(0, 1) if own else range(1, Y)

        def add(i):
            for r in blocks:
                sx[c, i, r] = (
                    gw[c, i, r, x].astype(F32) + rxc[c, 0, i, r].astype(F32) + rxc[c, 1, i, r].astype(F32)
                ).astype(BF)

        loop(0, Z, add)

    def rs_y_copy(c, d):
        to = (dp, z * Y + lax.rem(y + d, Y))
        return remote(sx.at[c, :, d], ry.at[c, d - 1], s_rs.at[11 + d, c], r_rs.at[11 + d, c], to)

    def rs_y(c):
        sum_x(c, False)
        for d in near:
            rs_y_copy(c, d).start()

    def rs_z(c):
        sum_x(c, True)
        for d in near:
            rs_y_copy(c, d).wait_recv()

        def sum_y(i):
            total = sx[c, i, 0].astype(F32)
            for d in range(Y - 1):
                total = total + ry[c, d, i].astype(F32)
            sy[c, i] = total.astype(BF)

        loop(0, Z, sum_y)

        def send(d):
            zz = lax.rem(z + d, Z)
            remote(
                sy.at[c, zz], rz.at[c, d - 1], s_rs.at[11 + Y, c], r_rs.at[11 + Y, c], (dp, zz * Y + y)
            ).start()

        loop(1, Z, send)

    def rs_z_desc(c):
        return remote(rz.at[c], rz.at[c], s_rs.at[11 + Y, c], r_rs.at[11 + Y, c], pdev)

    def rs_sum(c):
        rs_z_desc(c).wait_recv()
        total = sy[c, z].astype(F32)
        for d in range(Z - 1):
            total = total + rz[c, d].astype(F32)
        fin[:, cols(c)] = total.astype(BF)

    def field_rows(c):
        a2a_desc(3, c).wait_recv()
        front = mm(a4[...], got(3, c)) + skip[:, mine(c)] * p[c].reshape(M, CW).astype(F32)
        pgo[c] = front.astype(BF).reshape(2, rows, CW)

    out_pre = [local(pgo.at[c, h], pre.at[:, mine(c)], 4 + NC + c) for c in range(NC)]
    c_pre = [
        remote(pgo.at[c, other], pre.at[:, mine(c)], s_pair.at[NC + 2 + c], r_pair.at[NC + 2 + c], pdev)
        for c in range(NC)
    ]

    in_kern.wait()
    for c in range(NC):
        back_columns(c)
        ag_x2(c)
        a2a_start(1, c)
    in_tok.wait()
    c_tok.wait_recv()
    project(0)

    a2a_desc(1, 0).wait_recv()
    gradient_rows(0)
    rs_x1(0)
    a2a_start(2, 0)
    for c in range(1, NC):
        project(c)
        rs_x2(c - 1)
        a2a_desc(1, c).wait_recv()
        gradient_rows(c)
        rs_x1(c)
        a2a_start(2, c)

    def token_rows(i, b):
        total = mm_tb(gp[0, b], wb[0, i].reshape(TI, CW))
        for c in range(1, NC):
            total = total + mm_tb(gp[c, b], wb[c, i].reshape(TI, CW))
        return total.astype(BF)

    def gt_other(i):
        gts[:, pl.ds(pl.multiple_of(i * TI, TI), TI)] = token_rows(i, other)

    loop(0, Z, gt_other)
    c_gt = remote(gts, gtr, s_pair.at[NC + 1], r_pair.at[NC + 1], pdev)
    c_gt.start()

    rs_x3(0)
    forward_columns(0)
    rs_x2(NC - 1)
    a2a_start_odd(3, 0)
    rs_y(0)
    a2a_start_even(3, 0)
    rs_x3(NC - 1)
    for c in range(1, NC):
        forward_columns(c)
        rs_z(c - 1)
        a2a_start_odd(3, c)
        rs_y(c)
    a2a_start_even(3, NC - 1)

    def gt_own(i):
        gto[:, pl.ds(pl.multiple_of(i * TI, TI), TI)] = token_rows(i, h)

    loop(0, Z, gt_own)
    out_gt = local(gto, gtown, 4 + 2 * NC)
    out_gt.start()

    for c in range(NC - 1):
        rs_sum(c)
        field_rows(c)
        out_pre[c].start()
        c_pre[c].start()
    rs_z(NC - 1)
    rs_sum(NC - 1)
    my_rows = gfin.at[dp]

    def share(d):
        remote(fin, my_rows, s_rs.at[12 + Y, 0], r_rs.at[12 + Y, 0], (lax.rem(dp + d, DP), k)).start()

    loop(1, DP, share)
    out_fin = local(fin, my_rows, 5 + 2 * NC)
    out_fin.start()
    field_rows(NC - 1)
    out_pre[NC - 1].start()
    c_pre[NC - 1].start()
    share_desc = remote(
        gfin.at[pl.ds(0, DP - 1)], gfin.at[pl.ds(0, DP - 1)], s_rs.at[12 + Y, 0], r_rs.at[12 + Y, 0], pdev
    )

    for c in range(NC):
        out_pre[c].wait()
        c_pre[c].wait()
        c_g[c].wait_send()
        for copy in (c_xr2[c], c_xl2[c], ag_z_desc(c)):
            copy.wait_send()
        for d in range(Y):
            for copy in ag_x1_copies(c, d):
                copy.wait_send()
        for d in near:
            ag_y_copy(c, d).wait_send()
        for copy in rs_copies(c, False) + rs_copies(c, True):
            copy.wait_send()
        for d in near:
            rs_y_copy(c, d).wait_send()
        rs_z_desc(c).wait_send()
        for ph in range(4):
            a2a_desc(ph, c).wait_send()
    c_tok.wait_send()
    c_gt.wait()
    out_gt.wait()
    out_fin.wait()
    share_desc.wait()


def finish(pre, gate, cot, gtown, gtr, gfin, mixed, gtok, ggate, gwt):
    front = pre[...].astype(F32)
    mixed[...] = (gate[...].astype(F32) * front).astype(BF)
    ggate[...] = (cot[...].astype(F32) * front).astype(BF)
    gtok[...] = (gtown[...].astype(F32) + gtr[...].astype(F32)).astype(BF)
    HC = gfin.shape[2]
    for j in range(2):
        gwt[0, :, j * HC:(j + 1) * HC] = gfin[j].astype(F32)


def per_device(Y, CTX, tokens, weight, gate, skip, first, second, kern, third, fourth, cotangent):
    _, rows, D = tokens.shape
    HC = D // 2
    CW = HC // NC
    Z = CTX // Y
    M = 2 * rows
    CH = M // CTX
    R = first.shape[1]
    SL, Q = second.shape[0], second.shape[1]
    WR = D // CTX // X
    vm = pl.BlockSpec(memory_space=pltpu.VMEM)
    hbm = pl.BlockSpec(memory_space=pl.ANY)
    pre, gtown, gtr, gfin = pl.pallas_call(
        functools.partial(kernel, Y),
        out_shape=(
            pltpu.VMEM((rows, D), BF),
            pltpu.VMEM((rows, D), BF),
            pltpu.VMEM((rows, D), BF),
            pltpu.VMEM((2 * X, WR, HC), BF),
        ),
        in_specs=[hbm] * 10,
        out_specs=(vm,) * 4,
        scratch_shapes=[
            pltpu.VMEM((first.shape[0], R, R), BF),
            pltpu.VMEM((SL, Q, Q), BF),
            pltpu.VMEM((SL, Q, Q), BF),
            pltpu.VMEM((first.shape[0], R, R), BF),
            pltpu.VMEM((1, D), F32),
            pltpu.VMEM((M, M), BF),
            pltpu.VMEM((rows, D), BF),
            pltpu.VMEM((rows, D), BF),
            pltpu.VMEM((rows, D), BF),
            pltpu.VMEM((rows, D), BF),
            pltpu.VMEM((Q, SL, HC), BF),
            pltpu.VMEM((NC, 2, rows, CW), BF),
            pltpu.VMEM((NC, rows, CW), BF),
            pltpu.VMEM((NC, 2, rows, CW), BF),
            pltpu.VMEM((NC, 2, rows, CW), BF),
            pltpu.VMEM((NC, Z, Y, X, WR, CW), BF),
            pltpu.VMEM((NC, Z, Y, X, WR, CW), BF),
            pltpu.VMEM((4, NC, CTX, CH, CW), BF),
            pltpu.VMEM((4, NC, CTX, CH, CW), BF),
            pltpu.VMEM((NC, 2, Z // 2, Y, WR, CW), BF),
            pltpu.VMEM((NC, 2, Z, Y, WR, CW), BF),
            pltpu.VMEM((NC, Z, Y, WR, CW), BF),
            pltpu.VMEM((NC, Y - 1, Z, WR, CW), BF),
            pltpu.VMEM((NC, Z, WR, CW), BF),
            pltpu.VMEM((NC, Z - 1, WR, CW), BF),
            pltpu.VMEM((WR, HC), BF),
            pltpu.VMEM((M, M), BF),
            pltpu.VMEM((M, M), BF),
            pltpu.VMEM((M, M), BF),
            pltpu.VMEM((M, M), BF),
            pltpu.VMEM((SL * Q, M), BF),
            pltpu.VMEM((rows, D), BF),
            pltpu.VMEM((rows, D), BF),
            pltpu.VMEM((NC, 2, rows, CW), BF),
            pltpu.SemaphoreType.DMA((3 * Y + 2, NC)),
            pltpu.SemaphoreType.DMA((3 * Y + 2, NC)),
            pltpu.SemaphoreType.DMA((2 * NC + 2,)),
            pltpu.SemaphoreType.DMA((2 * NC + 2,)),
            pltpu.SemaphoreType.DMA((4, NC)),
            pltpu.SemaphoreType.DMA((4, NC)),
            pltpu.SemaphoreType.DMA((13 + Y, NC)),
            pltpu.SemaphoreType.DMA((13 + Y, NC)),
            pltpu.SemaphoreType.DMA((2 * NC + 11,)),
        ],
        compiler_params=pltpu.CompilerParams(
            collective_id=0, has_side_effects=True, vmem_limit_bytes=52 * 1024 * 1024
        ),
        cost_estimate=pl.CostEstimate(
            flops=8 * rows * D * D, bytes_accessed=8 * rows * D * 2, transcendentals=0
        ),
    )(
        tokens[0],
        weight.reshape(X, WR, D),
        gate[0],
        skip.reshape(1, D),
        first,
        second,
        kern,
        third,
        fourth,
        cotangent[0],
    )
    block = pl.BlockSpec((rows // X, D), lambda i: (i, 0))
    wide = pl.BlockSpec((1, WR, D), lambda i: (i, 0, 0))
    two = pl.BlockSpec((2, WR, HC), lambda i: (i, 0, 0))
    mixed, gtok, ggate, gwt = pl.pallas_call(
        finish,
        grid=(X,),
        out_shape=(
            jax.ShapeDtypeStruct((rows, D), BF),
            jax.ShapeDtypeStruct((rows, D), BF),
            jax.ShapeDtypeStruct((rows, D), BF),
            jax.ShapeDtypeStruct((X, WR, D), F32),
        ),
        in_specs=[block, block, block, block, block, two],
        out_specs=(block, block, block, wide),
        compiler_params=pltpu.CompilerParams(vmem_limit_bytes=16 * 1024 * 1024),
        cost_estimate=pl.CostEstimate(
            flops=8 * rows * D, bytes_accessed=16 * rows * D, transcendentals=0
        ),
    )(pre, gate[0], cotangent[0], gtown, gtr, gfin)
    return mixed[None], gtok[None], ggate[None], gwt.reshape(X * WR, D)


def solution(mesh, y_size=4):
    in_specs = (
        P("dp", "context", None),
        P("context", None),
        P("dp", "context", None),
        P(),
        P("context", None, None),
        P("context", None, None),
        P(None, "context", None),
        P("context", None, None),
        P("context", None, None),
        P("dp", "context", None),
    )
    out_specs = (
        P("dp", "context", None),
        P("dp", "context", None),
        P("dp", "context", None),
        P("context", None),
    )
    return jax.shard_map(
        functools.partial(per_device, y_size, mesh.shape["context"]),
        mesh=mesh, in_specs=in_specs, out_specs=out_specs, check_vma=False,
    )
```

```python
import functools

import jax
import jax.numpy as jnp
from jax import lax
from jax.experimental import pallas as pl
from jax.experimental.pallas import tpu as pltpu
from jax.sharding import PartitionSpec as P

BF = jnp.bfloat16
F32 = jnp.float32
MESH = pl.DeviceIdType.MESH
X = 4
NC = 2


def mm(a, b):
    return jnp.dot(a, b, preferred_element_type=F32)


def mm_ta(a, b):
    return lax.dot_general(a, b, (((0,), (0,)), ((), ())), preferred_element_type=F32)


def mm_tb(a, b):
    return lax.dot_general(a, b, (((1,), (1,)), ((), ())), preferred_element_type=F32)


def iota(shape, dim):
    return lax.broadcasted_iota(jnp.int32, shape, dim)


def ones_where(cond):
    return jnp.where(cond, 1.0, 0.0).astype(BF)


def loop(lo, hi, body):
    lax.fori_loop(lo, hi, lambda i, c: (body(i), c)[1], 0)


def kernel(
    Y,
    tok, wgt, gate, skip_in, f1_in, f2_in, kern, f3_in, f4_in, cot,
    pre, gtown, gtr, gfin,
    f1, f2, f3, f4, skip, a4, tk, tother, gv, cv, kv, g, gx, gp, p, wb, gw, sb, rb, rxa, rxc, sx, ry, sy, rz, fin,
    a1, a2, a3t, a4t, u, gts, gto, pgo,
    s_ag, r_ag, s_pair, r_pair, s_a2a, r_a2a, s_rs, r_rs, s_loc,
):
    dp = lax.axis_index("dp")
    k = lax.axis_index("context")
    DP = 2 * X
    Z = wb.shape[1]
    CTX = Z * Y
    h, x = lax.rem(dp, 2), lax.div(dp, 2)
    z, y = lax.div(k, Y), lax.rem(k, Y)
    right, left = lax.rem(x + 1, X), lax.rem(x + X - 1, X)
    opp = lax.rem(x + 2, X)
    other = 1 - h
    pair = x * 2 + other
    rows, D = tok.shape
    HC = D // 2
    QL, R = f1.shape[0], f1.shape[1]
    SL, Q = f2.shape[0], f2.shape[1]
    M = 2 * rows
    CH = M // CTX
    CW = HC // NC
    WR = wb.shape[4]
    half = pl.multiple_of(h * HC, HC)
    ohalf = pl.multiple_of(other * HC, HC)
    ZH = Z // 2
    TI = D // Z
    rdev, ldev, pdev = (right * 2 + h, k), (left * 2 + h, k), (pair, k)

    def remote(src, dst, ss, rs, dev):
        return pltpu.make_async_remote_copy(
            src_ref=src, dst_ref=dst, send_sem=ss, recv_sem=rs, device_id=dev, device_id_type=MESH
        )

    def local(src, dst, i):
        return pltpu.make_async_copy(src, dst, s_loc.at[i])

    def mine(c):
        return pl.ds(pl.multiple_of(h * HC + c * CW, CW), CW)

    def others(c):
        return pl.ds(pl.multiple_of(other * HC + c * CW, CW), CW)

    in_gate, in_cot = local(gate, gv, 0), local(cot, cv, 1)
    in_kern = local(kern.at[:, :, pl.ds(half, HC)], kv, 2)
    in_tok = local(tok, tk, 3)
    in_w = [local(wgt.at[x, :, mine(c)], wb.at[c, z, y, x], 4 + c) for c in range(NC)]
    small = [
        local(src, dst, 6 + 2 * NC + i)
        for i, (src, dst) in enumerate(
            ((f4_in, f4), (f3_in, f3), (f2_in, f2), (f1_in, f1), (skip_in, skip))
        )
    ]

    barrier = pltpu.get_barrier_semaphore()

    def greet_context(d):
        pl.semaphore_signal(barrier, inc=1, device_id=(dp, lax.rem(k + d, CTX)), device_id_type=MESH)

    def greet_dp(d):
        pl.semaphore_signal(barrier, inc=1, device_id=(lax.rem(dp + d, DP), k), device_id_type=MESH)

    loop(1, CTX, greet_context)
    loop(1, DP, greet_dp)
    in_gate.start()
    in_cot.start()
    for copy in small + in_w:
        copy.start()
    in_kern.start()
    in_tok.start()

    EB = 32
    in_gate.wait()
    in_cot.wait()

    def gate_rows(i):
        r = pl.ds(pl.multiple_of(i * EB, EB), EB)
        for c in range(NC):
            g[c, h, r, :] = (cv[r, mine(c)].astype(F32) * gv[r, mine(c)].astype(F32)).astype(BF)
            gx[c, r, :] = (cv[r, others(c)].astype(F32) * gv[r, others(c)].astype(F32)).astype(BF)

    loop(0, rows // EB, gate_rows)
    pl.semaphore_wait(barrier, CTX - 1 + DP - 1)

    c_g = [remote(gx.at[c], g.at[c, h], s_pair.at[c], r_pair.at[c], pdev) for c in range(NC)]
    for copy in c_g:
        copy.start()

    def ag_z(c):
        def send(d):
            zz = lax.rem(z + d, Z)
            remote(
                wgt.at[x, :, mine(c)], wb.at[c, z, y, x], s_ag.at[0, c], r_ag.at[0, c], (dp, zz * Y + y)
            ).start()

        loop(1, Z, send)

    def ag_z_desc(c):
        zs = pl.ds(0, Z - 1)
        return remote(wb.at[c, zs, y, x], wb.at[c, zs, y, x], s_ag.at[0, c], r_ag.at[0, c], pdev)

    for c in range(NC):
        ag_z(c)

    def row_matrix(dst, factor, transposed):
        rr, ss = iota((M, R), 0), iota((M, R), 1)
        for b in range(2):
            for q in range(QL):
                e = ones_where(rr == (ss // SL) * CH + b * (QL * SL) + q * SL + ss % SL)
                block = mm_tb(e, factor[q]) if transposed else mm(e, factor[q])
                dst[:, (b * QL + q) * R:(b * QL + q + 1) * R] = block.astype(BF)

    def column_matrix(dst, factor, transposed):
        qq, cc = iota((Q, M), 0), iota((Q, M), 1)
        for s in range(SL):
            e = ones_where(
                (cc // CH == qq // QL) & ((cc // SL) % QL == qq % QL) & (cc % SL == s)
            )
            block = mm_ta(factor[s], e) if transposed else mm(factor[s], e)
            u[s * Q:(s + 1) * Q, :] = block.astype(BF)
        rr, cc = iota((Q * SL, SL * Q), 0), iota((Q * SL, SL * Q), 1)
        move = ones_where((rr // SL == cc % Q) & (rr % SL == cc // Q))
        full = mm(move, u[...])
        owner = (iota((Q * SL, M), 1) // (QL * SL)) % 2
        for b in range(2):
            dst[b * Q * SL:(b + 1) * Q * SL, :] = jnp.where(owner == b, full, 0.0).astype(BF)

    def a2a_send(ph, c, lo, hi, step):
        def send(i):
            kk = lax.rem(k + i * step + 1, CTX)
            remote(
                sb.at[ph, c, kk], rb.at[ph, c, k], s_a2a.at[ph, c], r_a2a.at[ph, c], (dp, kk)
            ).start()

        loop(lo, hi, send)

    def a2a_start(ph, c):
        a2a_send(ph, c, 0, CTX - 1, 1)
        rb[ph, c, k] = sb[ph, c, k]

    def a2a_start_odd(ph, c):
        a2a_send(ph, c, 0, CTX // 2, 2)
        rb[ph, c, k] = sb[ph, c, k]

    def a2a_start_even(ph, c):
        def send(i):
            kk = lax.rem(k + 2 * i, CTX)
            remote(
                sb.at[ph, c, kk], rb.at[ph, c, k], s_a2a.at[ph, c], r_a2a.at[ph, c], (dp, kk)
            ).start()

        loop(1, CTX // 2, send)

    def a2a_desc(ph, c):
        most = pl.ds(0, CTX - 1)
        return remote(
            sb.at[ph, c, most], rb.at[ph, c, most], s_a2a.at[ph, c], r_a2a.at[ph, c],
            (dp, lax.rem(k + 1, CTX)),
        )

    def put(ph, c, value):
        sb[ph, c] = value.astype(BF).reshape(CTX, CH, CW)

    def got(ph, c):
        return rb[ph, c].reshape(M, CW)

    def cols(c):
        return slice(c * CW, (c + 1) * CW)

    small[0].wait()
    row_matrix(a4t, f4, True)

    near = sorted(range(1, Y), key=lambda d: min(d, Y - d))

    def ag_y_copy(c, d):
        to = (dp, z * Y + lax.rem(y + d, Y))
        return remote(wb.at[c, :, y, x], wb.at[c, :, y, x], s_ag.at[d, c], r_ag.at[d, c], to)

    def ag_x1_copies(c, d):
        block = wb.at[c, :, lax.rem(y - d + Y, Y), x]
        return (
            remote(block, block, s_ag.at[Y + d, c], r_ag.at[Y + d, c], rdev),
            remote(block, block, s_ag.at[2 * Y + d, c], r_ag.at[2 * Y + d, c], ldev),
        )

    def ag_x1_send(c, d):
        for copy in ag_x1_copies(c, d):
            copy.start()

    def ag_y(c):
        ag_z_desc(c).wait_recv()
        in_w[c].wait()
        for d in near:
            ag_y_copy(c, d).start()
        ag_x1_send(c, 0)

    for c in range(NC):
        c_g[c].wait_recv()
        put(0, c, mm(a4t[...], g[c].reshape(M, CW)))
        a2a_start(0, c)
        ag_y(c)
    c_tok = remote(tok, tother, s_pair.at[NC], r_pair.at[NC], pdev)
    c_tok.start()
    for copy in small[1:]:
        copy.wait()
    column_matrix(a3t, f3, True)

    lo, hi = pl.ds(0, ZH), pl.ds(ZH, Z - ZH)
    last = 3 * Y
    c_xr2 = [
        remote(wb.at[c, lo, :, left], wb.at[c, lo, :, left], s_ag.at[last, c], r_ag.at[last, c], rdev)
        for c in range(NC)
    ]
    c_xl2 = [
        remote(wb.at[c, hi, :, right], wb.at[c, hi, :, right], s_ag.at[last + 1, c], r_ag.at[last + 1, c], ldev)
        for c in range(NC)
    ]

    def ag_x1(c):
        for d in near:
            ag_y_copy(c, d).wait_recv()
            ag_x1_send(c, d)

    def ag_x2(c):
        for d in range(Y):
            ag_x1_copies(c, d)[0].wait_recv()
        c_xr2[c].start()
        for d in range(Y):
            ag_x1_copies(c, d)[1].wait_recv()
        c_xl2[c].start()

    ag_x1(0)
    column_matrix(a2, f2, False)
    for c in range(1, NC):
        ag_x1(c)
    row_matrix(a1, f1, False)
    a4[...] = a4t[...].T

    def filtered(value, c):
        kc = kv[:, :, cols(c)].astype(F32).reshape(Q * SL, CW)
        return (value.reshape(2, Q * SL, CW) * kc[None]).astype(BF).reshape(M, CW)

    def back_columns(c):
        a2a_desc(0, c).wait_recv()
        gs = filtered(mm(a3t[...], got(0, c)), c)
        put(1, c, mm_ta(a2[...], gs))

    def forward_columns(c):
        a2a_desc(2, c).wait_recv()
        fl = filtered(mm(a2[...], got(2, c)), c)
        put(3, c, mm_ta(a3t[...], fl))

    def project(c):
        c_xr2[c].wait_recv()
        c_xl2[c].wait_recv()
        wc = wb[c].reshape(D, CW)
        p[c, h] = mm(tk[...], wc).astype(BF)
        p[c, other] = mm(tother[...], wc).astype(BF)
        put(2, c, mm(a1[...], p[c].reshape(M, CW)))

    def gradient_rows(c):
        gf = mm_ta(a1[...], got(1, c)) + skip[:, mine(c)] * g[c].reshape(M, CW).astype(F32)
        gp[c] = gf.astype(BF).reshape(2, rows, CW)

    def rs_copies(c, own):
        yb = pl.ds(0, 1) if own else pl.ds(1, Y - 1)
        at = 6 if own else 0
        moves = (
            (gw.at[c, lo, yb, opp], rxa.at[c, 0, :, yb], rdev),
            (gw.at[c, hi, yb, opp], rxa.at[c, 1, :, yb], ldev),
            (gw.at[c, hi, yb, right], rxc.at[c, 0, hi, yb], rdev),
            (gw.at[c, lo, yb, left], rxc.at[c, 1, lo, yb], ldev),
            (gw.at[c, lo, yb, right], rxc.at[c, 0, lo, yb], rdev),
            (gw.at[c, hi, yb, left], rxc.at[c, 1, hi, yb], ldev),
        )
        return [
            remote(src, dst, s_rs.at[at + i, c], r_rs.at[at + i, c], dev)
            for i, (src, dst, dev) in enumerate(moves)
        ]

    def rs_x1(c):
        def part_rows(i):
            at = pl.ds(pl.multiple_of(i * TI, TI), TI)
            part = mm_ta(tk[:, at], gp[c, h]) + mm_ta(tother[:, at], gp[c, other])
            part = part.astype(BF).reshape(Y, X, WR, CW)
            for yy in range(Y):
                gw[c, i, lax.rem(yy - y + Y, Y)] = part[yy]

        loop(0, Z, part_rows)
        for copy in rs_copies(c, False)[:4]:
            copy.start()

    def rs_pass(c, own):
        copies = rs_copies(c, own)
        blocks = range(0, 1) if own else range(1, Y)

        def add_right(i):
            for r in blocks:
                gw[c, i, r, right] = (
                    gw[c, i, r, right].astype(F32) + rxa[c, 0, i, r].astype(F32)
                ).astype(BF)

        def add_left(i):
            for r in blocks:
                gw[c, ZH + i, r, left] = (
                    gw[c, ZH + i, r, left].astype(F32) + rxa[c, 1, i, r].astype(F32)
                ).astype(BF)

        copies[0].wait_recv()
        loop(0, ZH, add_right)
        copies[4].start()
        copies[1].wait_recv()
        loop(0, ZH, add_left)
        copies[5].start()

    def rs_x2(c):
        rs_pass(c, False)
        for copy in rs_copies(c, True)[:4]:
            copy.start()

    def rs_x3(c):
        rs_pass(c, True)

    def sum_x(c, own):
        for copy in rs_copies(c, own)[2:]:
            copy.wait_recv()
        blocks = range(0, 1) if own else range(1, Y)

        def add(i):
            for r in blocks:
                sx[c, i, r] = (
                    gw[c, i, r, x].astype(F32) + rxc[c, 0, i, r].astype(F32) + rxc[c, 1, i, r].astype(F32)
                ).astype(BF)

        loop(0, Z, add)

    def rs_y_copy(c, d):
        to = (dp, z * Y + lax.rem(y + d, Y))
        return remote(sx.at[c, :, d], ry.at[c, d - 1], s_rs.at[11 + d, c], r_rs.at[11 + d, c], to)

    def rs_y(c):
        sum_x(c, False)
        for d in near:
            rs_y_copy(c, d).start()

    def rs_z(c):
        sum_x(c, True)
        for d in near:
            rs_y_copy(c, d).wait_recv()

        def sum_y(i):
            total = sx[c, i, 0].astype(F32)
            for d in range(Y - 1):
                total = total + ry[c, d, i].astype(F32)
            sy[c, i] = total.astype(BF)

        loop(0, Z, sum_y)

        def send(d):
            zz = lax.rem(z + d, Z)
            remote(
                sy.at[c, zz], rz.at[c, d - 1], s_rs.at[11 + Y, c], r_rs.at[11 + Y, c], (dp, zz * Y + y)
            ).start()

        loop(1, Z, send)

    def rs_z_desc(c):
        return remote(rz.at[c], rz.at[c], s_rs.at[11 + Y, c], r_rs.at[11 + Y, c], pdev)

    def rs_sum(c):
        rs_z_desc(c).wait_recv()
        total = sy[c, z].astype(F32)
        for d in range(Z - 1):
            total = total + rz[c, d].astype(F32)
        fin[:, cols(c)] = total.astype(BF)

    def field_rows(c):
        a2a_desc(3, c).wait_recv()
        front = mm(a4[...], got(3, c)) + skip[:, mine(c)] * p[c].reshape(M, CW).astype(F32)
        pgo[c] = front.astype(BF).reshape(2, rows, CW)

    out_pre = [local(pgo.at[c, h], pre.at[:, mine(c)], 4 + NC + c) for c in range(NC)]
    c_pre = [
        remote(pgo.at[c, other], pre.at[:, mine(c)], s_pair.at[NC + 2 + c], r_pair.at[NC + 2 + c], pdev)
        for c in range(NC)
    ]

    in_kern.wait()
    for c in range(NC):
        back_columns(c)
        a2a_start_odd(1, c)
        ag_x2(c)
        a2a_start_even(1, c)
    in_tok.wait()
    c_tok.wait_recv()
    project(0)

    a2a_desc(1, 0).wait_recv()
    gradient_rows(0)
    rs_x1(0)
    a2a_start(2, 0)
    for c in range(1, NC):
        project(c)
        rs_x2(c - 1)
        a2a_desc(1, c).wait_recv()
        gradient_rows(c)
        rs_x1(c)
        a2a_start(2, c)

    def token_rows(i, b):
        total = mm_tb(gp[0, b], wb[0, i].reshape(TI, CW))
        for c in range(1, NC):
            total = total + mm_tb(gp[c, b], wb[c, i].reshape(TI, CW))
        return total.astype(BF)

    def gt_other(i):
        gts[:, pl.ds(pl.multiple_of(i * TI, TI), TI)] = token_rows(i, other)

    loop(0, Z, gt_other)
    c_gt = remote(gts, gtr, s_pair.at[NC + 1], r_pair.at[NC + 1], pdev)
    c_gt.start()

    rs_x3(0)
    forward_columns(0)
    rs_x2(NC - 1)
    a2a_start_odd(3, 0)
    rs_y(0)
    a2a_start_even(3, 0)
    rs_x3(NC - 1)

    def gt_own(i):
        gto[:, pl.ds(pl.multiple_of(i * TI, TI), TI)] = token_rows(i, h)

    loop(0, Z, gt_own)
    out_gt = local(gto, gtown, 4 + 2 * NC)
    out_gt.start()

    for c in range(1, NC):
        forward_columns(c)
        rs_z(c - 1)
        a2a_start_odd(3, c)
        rs_y(c)
    a2a_start_even(3, NC - 1)

    for c in range(NC - 1):
        rs_sum(c)
        field_rows(c)
        out_pre[c].start()
        c_pre[c].start()
    rs_z(NC - 1)
    field_rows(NC - 1)
    out_pre[NC - 1].start()
    c_pre[NC - 1].start()
    rs_sum(NC - 1)
    my_rows = gfin.at[dp]

    def share(d):
        remote(fin, my_rows, s_rs.at[12 + Y, 0], r_rs.at[12 + Y, 0], (lax.rem(dp + d, DP), k)).start()

    loop(1, DP, share)
    out_fin = local(fin, my_rows, 5 + 2 * NC)
    out_fin.start()
    share_desc = remote(
        gfin.at[pl.ds(0, DP - 1)], gfin.at[pl.ds(0, DP - 1)], s_rs.at[12 + Y, 0], r_rs.at[12 + Y, 0], pdev
    )

    for c in range(NC):
        out_pre[c].wait()
        c_pre[c].wait()
        c_g[c].wait_send()
        for copy in (c_xr2[c], c_xl2[c], ag_z_desc(c)):
            copy.wait_send()
        for d in range(Y):
            for copy in ag_x1_copies(c, d):
                copy.wait_send()
        for d in near:
            ag_y_copy(c, d).wait_send()
        for copy in rs_copies(c, False) + rs_copies(c, True):
            copy.wait_send()
        for d in near:
            rs_y_copy(c, d).wait_send()
        rs_z_desc(c).wait_send()
        for ph in range(4):
            a2a_desc(ph, c).wait_send()
    c_tok.wait_send()
    c_gt.wait()
    out_gt.wait()
    out_fin.wait()
    share_desc.wait()


def finish(pre, gate, cot, gtown, gtr, gfin, mixed, gtok, ggate, gwt, mv, tv, gv, wv, sems):
    rows, D = pre.shape
    HC = gfin.shape[2]
    part = rows // X
    copies = []
    for i in range(X):
        r = slice(i * part, (i + 1) * part)
        at = pl.ds(i * part, part)
        front = pre[r].astype(F32)
        mv[r] = (gate[r].astype(F32) * front).astype(BF)
        copies.append(pltpu.make_async_copy(mv.at[at], mixed.at[at], sems.at[4 * i]))
        copies[-1].start()
        gv[r] = (cot[r].astype(F32) * front).astype(BF)
        copies.append(pltpu.make_async_copy(gv.at[at], ggate.at[at], sems.at[4 * i + 1]))
        copies[-1].start()
        tv[r] = (gtown[r].astype(F32) + gtr[r].astype(F32)).astype(BF)
        copies.append(pltpu.make_async_copy(tv.at[at], gtok.at[at], sems.at[4 * i + 2]))
        copies[-1].start()
        for j in range(2):
            wv[i, :, j * HC:(j + 1) * HC] = gfin[2 * i + j].astype(F32)
        copies.append(pltpu.make_async_copy(wv.at[i], gwt.at[i], sems.at[4 * i + 3]))
        copies[-1].start()
    for copy in copies:
        copy.wait()


def per_device(Y, CTX, tokens, weight, gate, skip, first, second, kern, third, fourth, cotangent):
    _, rows, D = tokens.shape
    HC = D // 2
    CW = HC // NC
    Z = CTX // Y
    M = 2 * rows
    CH = M // CTX
    R = first.shape[1]
    SL, Q = second.shape[0], second.shape[1]
    WR = D // CTX // X
    vm = pl.BlockSpec(memory_space=pltpu.VMEM)
    hbm = pl.BlockSpec(memory_space=pl.ANY)
    pre, gtown, gtr, gfin = pl.pallas_call(
        functools.partial(kernel, Y),
        out_shape=(
            pltpu.VMEM((rows, D), BF),
            pltpu.VMEM((rows, D), BF),
            pltpu.VMEM((rows, D), BF),
            pltpu.VMEM((2 * X, WR, HC), BF),
        ),
        in_specs=[hbm] * 10,
        out_specs=(vm,) * 4,
        scratch_shapes=[
            pltpu.VMEM((first.shape[0], R, R), BF),
            pltpu.VMEM((SL, Q, Q), BF),
            pltpu.VMEM((SL, Q, Q), BF),
            pltpu.VMEM((first.shape[0], R, R), BF),
            pltpu.VMEM((1, D), F32),
            pltpu.VMEM((M, M), BF),
            pltpu.VMEM((rows, D), BF),
            pltpu.VMEM((rows, D), BF),
            pltpu.VMEM((rows, D), BF),
            pltpu.VMEM((rows, D), BF),
            pltpu.VMEM((Q, SL, HC), BF),
            pltpu.VMEM((NC, 2, rows, CW), BF),
            pltpu.VMEM((NC, rows, CW), BF),
            pltpu.VMEM((NC, 2, rows, CW), BF),
            pltpu.VMEM((NC, 2, rows, CW), BF),
            pltpu.VMEM((NC, Z, Y, X, WR, CW), BF),
            pltpu.VMEM((NC, Z, Y, X, WR, CW), BF),
            pltpu.VMEM((4, NC, CTX, CH, CW), BF),
            pltpu.VMEM((4, NC, CTX, CH, CW), BF),
            pltpu.VMEM((NC, 2, Z // 2, Y, WR, CW), BF),
            pltpu.VMEM((NC, 2, Z, Y, WR, CW), BF),
            pltpu.VMEM((NC, Z, Y, WR, CW), BF),
            pltpu.VMEM((NC, Y - 1, Z, WR, CW), BF),
            pltpu.VMEM((NC, Z, WR, CW), BF),
            pltpu.VMEM((NC, Z - 1, WR, CW), BF),
            pltpu.VMEM((WR, HC), BF),
            pltpu.VMEM((M, M), BF),
            pltpu.VMEM((M, M), BF),
            pltpu.VMEM((M, M), BF),
            pltpu.VMEM((M, M), BF),
            pltpu.VMEM((SL * Q, M), BF),
            pltpu.VMEM((rows, D), BF),
            pltpu.VMEM((rows, D), BF),
            pltpu.VMEM((NC, 2, rows, CW), BF),
            pltpu.SemaphoreType.DMA((3 * Y + 2, NC)),
            pltpu.SemaphoreType.DMA((3 * Y + 2, NC)),
            pltpu.SemaphoreType.DMA((2 * NC + 2,)),
            pltpu.SemaphoreType.DMA((2 * NC + 2,)),
            pltpu.SemaphoreType.DMA((4, NC)),
            pltpu.SemaphoreType.DMA((4, NC)),
            pltpu.SemaphoreType.DMA((13 + Y, NC)),
            pltpu.SemaphoreType.DMA((13 + Y, NC)),
            pltpu.SemaphoreType.DMA((2 * NC + 11,)),
        ],
        compiler_params=pltpu.CompilerParams(
            collective_id=0, has_side_effects=True, vmem_limit_bytes=52 * 1024 * 1024
        ),
        cost_estimate=pl.CostEstimate(
            flops=8 * rows * D * D, bytes_accessed=8 * rows * D * 2, transcendentals=0
        ),
    )(
        tokens[0],
        weight.reshape(X, WR, D),
        gate[0],
        skip.reshape(1, D),
        first,
        second,
        kern,
        third,
        fourth,
        cotangent[0],
    )
    mixed, gtok, ggate, gwt = pl.pallas_call(
        finish,
        out_shape=(
            jax.ShapeDtypeStruct((rows, D), BF),
            jax.ShapeDtypeStruct((rows, D), BF),
            jax.ShapeDtypeStruct((rows, D), BF),
            jax.ShapeDtypeStruct((X, WR, D), F32),
        ),
        in_specs=[vm] * 6,
        out_specs=(hbm,) * 4,
        scratch_shapes=[
            pltpu.VMEM((rows, D), BF),
            pltpu.VMEM((rows, D), BF),
            pltpu.VMEM((rows, D), BF),
            pltpu.VMEM((X, WR, D), F32),
            pltpu.SemaphoreType.DMA((4 * X,)),
        ],
        compiler_params=pltpu.CompilerParams(vmem_limit_bytes=16 * 1024 * 1024),
        cost_estimate=pl.CostEstimate(
            flops=8 * rows * D, bytes_accessed=16 * rows * D, transcendentals=0
        ),
    )(pre, gate[0], cotangent[0], gtown, gtr, gfin)
    return mixed[None], gtok[None], ggate[None], gwt.reshape(X * WR, D)


def solution(mesh, y_size=4):
    in_specs = (
        P("dp", "context", None),
        P("context", None),
        P("dp", "context", None),
        P(),
        P("context", None, None),
        P("context", None, None),
        P(None, "context", None),
        P("context", None, None),
        P("context", None, None),
        P("dp", "context", None),
    )
    out_specs = (
        P("dp", "context", None),
        P("dp", "context", None),
        P("dp", "context", None),
        P("context", None),
    )
    return jax.shard_map(
        functools.partial(per_device, y_size, mesh.shape["context"]),
        mesh=mesh, in_specs=in_specs, out_specs=out_specs, check_vma=False,
    )
```

```python
import functools

import jax
import jax.numpy as jnp
from jax import lax
from jax.experimental import pallas as pl
from jax.experimental.pallas import tpu as pltpu
from jax.sharding import PartitionSpec as P

BF = jnp.bfloat16
F32 = jnp.float32
MESH = pl.DeviceIdType.MESH
X = 4
NC = 2


def mm(a, b):
    return jnp.dot(a, b, preferred_element_type=F32)


def mm_ta(a, b):
    return lax.dot_general(a, b, (((0,), (0,)), ((), ())), preferred_element_type=F32)


def mm_tb(a, b):
    return lax.dot_general(a, b, (((1,), (1,)), ((), ())), preferred_element_type=F32)


def iota(shape, dim):
    return lax.broadcasted_iota(jnp.int32, shape, dim)


def ones_where(cond):
    return jnp.where(cond, 1.0, 0.0).astype(BF)


def loop(lo, hi, body):
    lax.fori_loop(lo, hi, lambda i, c: (body(i), c)[1], 0)


def kernel(
    Y,
    tok, wgt, gate, skip_in, f1_in, f2_in, kern, f3_in, f4_in, cot,
    pre, gtown, gtr, gfin,
    f1, f2, f3, f4, skip, a4, tk, tother, gv, cv, kv, g, gx, gp, p, wb, gw, sb, rb, rxa, rxc, sx, ry, sy, rz, fin,
    a1, a2, a3t, a4t, u, gts, gto, pgo,
    s_ag, r_ag, s_pair, r_pair, s_a2a, r_a2a, s_rs, r_rs, s_loc,
):
    dp = lax.axis_index("dp")
    k = lax.axis_index("context")
    DP = 2 * X
    Z = wb.shape[1]
    CTX = Z * Y
    h, x = lax.rem(dp, 2), lax.div(dp, 2)
    z, y = lax.div(k, Y), lax.rem(k, Y)
    right, left = lax.rem(x + 1, X), lax.rem(x + X - 1, X)
    opp = lax.rem(x + 2, X)
    other = 1 - h
    pair = x * 2 + other
    rows, D = tok.shape
    HC = D // 2
    QL, R = f1.shape[0], f1.shape[1]
    SL, Q = f2.shape[0], f2.shape[1]
    M = 2 * rows
    CH = M // CTX
    CW = HC // NC
    WR = wb.shape[4]
    half = pl.multiple_of(h * HC, HC)
    ohalf = pl.multiple_of(other * HC, HC)
    ZH = Z // 2
    TI = D // Z
    rdev, ldev, pdev = (right * 2 + h, k), (left * 2 + h, k), (pair, k)

    def remote(src, dst, ss, rs, dev):
        return pltpu.make_async_remote_copy(
            src_ref=src, dst_ref=dst, send_sem=ss, recv_sem=rs, device_id=dev, device_id_type=MESH
        )

    def local(src, dst, i):
        return pltpu.make_async_copy(src, dst, s_loc.at[i])

    def mine(c):
        return pl.ds(pl.multiple_of(h * HC + c * CW, CW), CW)

    def others(c):
        return pl.ds(pl.multiple_of(other * HC + c * CW, CW), CW)

    in_gate, in_cot = local(gate, gv, 0), local(cot, cv, 1)
    in_kern = local(kern.at[:, :, pl.ds(half, HC)], kv, 2)
    in_tok = local(tok, tk, 3)
    in_w = [local(wgt.at[x, :, mine(c)], wb.at[c, z, y, x], 4 + c) for c in range(NC)]
    small = [
        local(src, dst, 6 + 2 * NC + i)
        for i, (src, dst) in enumerate(
            ((f4_in, f4), (f3_in, f3), (f2_in, f2), (f1_in, f1), (skip_in, skip))
        )
    ]

    barrier = pltpu.get_barrier_semaphore()

    def greet_context(d):
        pl.semaphore_signal(barrier, inc=1, device_id=(dp, lax.rem(k + d, CTX)), device_id_type=MESH)

    def greet_dp(d):
        pl.semaphore_signal(barrier, inc=1, device_id=(lax.rem(dp + d, DP), k), device_id_type=MESH)

    loop(1, CTX, greet_context)
    loop(1, DP, greet_dp)
    in_gate.start()
    in_cot.start()
    for copy in small + in_w:
        copy.start()
    in_kern.start()
    in_tok.start()

    EB = 32
    in_gate.wait()
    in_cot.wait()

    def gate_rows(i):
        r = pl.ds(pl.multiple_of(i * EB, EB), EB)
        for c in range(NC):
            g[c, h, r, :] = (cv[r, mine(c)].astype(F32) * gv[r, mine(c)].astype(F32)).astype(BF)
            gx[c, r, :] = (cv[r, others(c)].astype(F32) * gv[r, others(c)].astype(F32)).astype(BF)

    loop(0, rows // EB, gate_rows)
    pl.semaphore_wait(barrier, CTX - 1 + DP - 1)

    c_g = [remote(gx.at[c], g.at[c, h], s_pair.at[c], r_pair.at[c], pdev) for c in range(NC)]
    for copy in c_g:
        copy.start()

    def ag_z(c):
        def send(d):
            zz = lax.rem(z + d, Z)
            remote(
                wgt.at[x, :, mine(c)], wb.at[c, z, y, x], s_ag.at[0, c], r_ag.at[0, c], (dp, zz * Y + y)
            ).start()

        loop(1, Z, send)

    def ag_z_desc(c):
        zs = pl.ds(0, Z - 1)
        return remote(wb.at[c, zs, y, x], wb.at[c, zs, y, x], s_ag.at[0, c], r_ag.at[0, c], pdev)

    for c in range(NC):
        ag_z(c)

    def row_matrix(dst, factor, transposed):
        rr, ss = iota((M, R), 0), iota((M, R), 1)
        for b in range(2):
            for q in range(QL):
                e = ones_where(rr == (ss // SL) * CH + b * (QL * SL) + q * SL + ss % SL)
                block = mm_tb(e, factor[q]) if transposed else mm(e, factor[q])
                dst[:, (b * QL + q) * R:(b * QL + q + 1) * R] = block.astype(BF)

    def column_matrix(dst, factor, transposed):
        qq, cc = iota((Q, M), 0), iota((Q, M), 1)
        for s in range(SL):
            e = ones_where(
                (cc // CH == qq // QL) & ((cc // SL) % QL == qq % QL) & (cc % SL == s)
            )
            block = mm_ta(factor[s], e) if transposed else mm(factor[s], e)
            u[s * Q:(s + 1) * Q, :] = block.astype(BF)
        rr, cc = iota((Q * SL, SL * Q), 0), iota((Q * SL, SL * Q), 1)
        move = ones_where((rr // SL == cc % Q) & (rr % SL == cc // Q))
        full = mm(move, u[...])
        owner = (iota((Q * SL, M), 1) // (QL * SL)) % 2
        for b in range(2):
            dst[b * Q * SL:(b + 1) * Q * SL, :] = jnp.where(owner == b, full, 0.0).astype(BF)

    def a2a_send(ph, c, lo, hi, step):
        def send(i):
            kk = lax.rem(k + i * step + 1, CTX)
            remote(
                sb.at[ph, c, kk], rb.at[ph, c, k], s_a2a.at[ph, c], r_a2a.at[ph, c], (dp, kk)
            ).start()

        loop(lo, hi, send)

    def a2a_start(ph, c):
        a2a_send(ph, c, 0, CTX - 1, 1)
        rb[ph, c, k] = sb[ph, c, k]

    def a2a_start_odd(ph, c):
        a2a_send(ph, c, 0, CTX // 2, 2)
        rb[ph, c, k] = sb[ph, c, k]

    def a2a_start_even(ph, c):
        def send(i):
            kk = lax.rem(k + 2 * i, CTX)
            remote(
                sb.at[ph, c, kk], rb.at[ph, c, k], s_a2a.at[ph, c], r_a2a.at[ph, c], (dp, kk)
            ).start()

        loop(1, CTX // 2, send)

    def a2a_desc(ph, c):
        most = pl.ds(0, CTX - 1)
        return remote(
            sb.at[ph, c, most], rb.at[ph, c, most], s_a2a.at[ph, c], r_a2a.at[ph, c],
            (dp, lax.rem(k + 1, CTX)),
        )

    def put(ph, c, value):
        sb[ph, c] = value.astype(BF).reshape(CTX, CH, CW)

    def got(ph, c):
        return rb[ph, c].reshape(M, CW)

    def cols(c):
        return slice(c * CW, (c + 1) * CW)

    small[0].wait()
    row_matrix(a4t, f4, True)

    near = sorted(range(1, Y), key=lambda d: min(d, Y - d))

    def ag_y_copy(c, d):
        to = (dp, z * Y + lax.rem(y + d, Y))
        return remote(wb.at[c, :, y, x], wb.at[c, :, y, x], s_ag.at[d, c], r_ag.at[d, c], to)

    def ag_x1_copies(c, d):
        block = wb.at[c, :, lax.rem(y - d + Y, Y), x]
        return (
            remote(block, block, s_ag.at[Y + d, c], r_ag.at[Y + d, c], rdev),
            remote(block, block, s_ag.at[2 * Y + d, c], r_ag.at[2 * Y + d, c], ldev),
        )

    def ag_x1_send(c, d):
        for copy in ag_x1_copies(c, d):
            copy.start()

    def ag_y(c):
        ag_z_desc(c).wait_recv()
        in_w[c].wait()
        for d in near:
            ag_y_copy(c, d).start()
        ag_x1_send(c, 0)

    for c in range(NC):
        c_g[c].wait_recv()
        put(0, c, mm(a4t[...], g[c].reshape(M, CW)))
        a2a_start(0, c)
        ag_y(c)
    c_tok = remote(tok, tother, s_pair.at[NC], r_pair.at[NC], pdev)
    c_tok.start()
    for copy in small[1:]:
        copy.wait()
    column_matrix(a3t, f3, True)

    lo, hi = pl.ds(0, ZH), pl.ds(ZH, Z - ZH)
    last = 3 * Y
    c_xr2 = [
        remote(wb.at[c, lo, :, left], wb.at[c, lo, :, left], s_ag.at[last, c], r_ag.at[last, c], rdev)
        for c in range(NC)
    ]
    c_xl2 = [
        remote(wb.at[c, hi, :, right], wb.at[c, hi, :, right], s_ag.at[last + 1, c], r_ag.at[last + 1, c], ldev)
        for c in range(NC)
    ]

    def ag_x1(c):
        for d in near:
            ag_y_copy(c, d).wait_recv()
            ag_x1_send(c, d)

    def ag_x2(c):
        for d in range(Y):
            ag_x1_copies(c, d)[0].wait_recv()
        c_xr2[c].start()
        for d in range(Y):
            ag_x1_copies(c, d)[1].wait_recv()
        c_xl2[c].start()

    ag_x1(0)
    column_matrix(a2, f2, False)
    for c in range(1, NC):
        ag_x1(c)
    row_matrix(a1, f1, False)
    a4[...] = a4t[...].T

    def filtered(value, c):
        kc = kv[:, :, cols(c)].astype(F32).reshape(Q * SL, CW)
        return (value.reshape(2, Q * SL, CW) * kc[None]).astype(BF).reshape(M, CW)

    def back_columns(c):
        a2a_desc(0, c).wait_recv()
        gs = filtered(mm(a3t[...], got(0, c)), c)
        put(1, c, mm_ta(a2[...], gs))

    def forward_columns(c):
        a2a_desc(2, c).wait_recv()
        fl = filtered(mm(a2[...], got(2, c)), c)
        put(3, c, mm_ta(a3t[...], fl))

    def project(c):
        c_xr2[c].wait_recv()
        c_xl2[c].wait_recv()
        wc = wb[c].reshape(D, CW)
        p[c, h] = mm(tk[...], wc).astype(BF)
        p[c, other] = mm(tother[...], wc).astype(BF)
        put(2, c, mm(a1[...], p[c].reshape(M, CW)))

    def gradient_rows(c):
        gf = mm_ta(a1[...], got(1, c)) + skip[:, mine(c)] * g[c].reshape(M, CW).astype(F32)
        gp[c] = gf.astype(BF).reshape(2, rows, CW)

    def rs_copies(c, own):
        yb = pl.ds(0, 1) if own else pl.ds(1, Y - 1)
        at = 6 if own else 0
        moves = (
            (gw.at[c, lo, yb, opp], rxa.at[c, 0, :, yb], rdev),
            (gw.at[c, hi, yb, opp], rxa.at[c, 1, :, yb], ldev),
            (gw.at[c, hi, yb, right], rxc.at[c, 0, hi, yb], rdev),
            (gw.at[c, lo, yb, left], rxc.at[c, 1, lo, yb], ldev),
            (gw.at[c, lo, yb, right], rxc.at[c, 0, lo, yb], rdev),
            (gw.at[c, hi, yb, left], rxc.at[c, 1, hi, yb], ldev),
        )
        return [
            remote(src, dst, s_rs.at[at + i, c], r_rs.at[at + i, c], dev)
            for i, (src, dst, dev) in enumerate(moves)
        ]

    def rs_x1(c):
        def part_rows(i):
            at = pl.ds(pl.multiple_of(i * TI, TI), TI)
            part = mm_ta(tk[:, at], gp[c, h]) + mm_ta(tother[:, at], gp[c, other])
            part = part.astype(BF).reshape(Y, X, WR, CW)
            for yy in range(Y):
                gw[c, i, lax.rem(yy - y + Y, Y)] = part[yy]

        loop(0, Z, part_rows)
        for copy in rs_copies(c, False)[:4]:
            copy.start()

    def rs_pass(c, own):
        copies = rs_copies(c, own)
        blocks = range(0, 1) if own else range(1, Y)

        def add_right(i):
            for r in blocks:
                gw[c, i, r, right] = (
                    gw[c, i, r, right].astype(F32) + rxa[c, 0, i, r].astype(F32)
                ).astype(BF)

        def add_left(i):
            for r in blocks:
                gw[c, ZH + i, r, left] = (
                    gw[c, ZH + i, r, left].astype(F32) + rxa[c, 1, i, r].astype(F32)
                ).astype(BF)

        copies[0].wait_recv()
        loop(0, ZH, add_right)
        copies[4].start()
        copies[1].wait_recv()
        loop(0, ZH, add_left)
        copies[5].start()

    def rs_x2(c):
        rs_pass(c, False)
        for copy in rs_copies(c, True)[:4]:
            copy.start()

    def rs_x3(c):
        rs_pass(c, True)

    def sum_x(c, own):
        for copy in rs_copies(c, own)[2:]:
            copy.wait_recv()
        blocks = range(0, 1) if own else range(1, Y)

        def add(i):
            for r in blocks:
                sx[c, i, r] = (
                    gw[c, i, r, x].astype(F32) + rxc[c, 0, i, r].astype(F32) + rxc[c, 1, i, r].astype(F32)
                ).astype(BF)

        loop(0, Z, add)

    def rs_y_copy(c, d):
        to = (dp, z * Y + lax.rem(y + d, Y))
        return remote(sx.at[c, :, d], ry.at[c, d - 1], s_rs.at[11 + d, c], r_rs.at[11 + d, c], to)

    def rs_y(c):
        sum_x(c, False)
        for d in near:
            rs_y_copy(c, d).start()

    def rs_z(c):
        sum_x(c, True)
        for d in near:
            rs_y_copy(c, d).wait_recv()

        def sum_y(i):
            total = sx[c, i, 0].astype(F32)
            for d in range(Y - 1):
                total = total + ry[c, d, i].astype(F32)
            sy[c, i] = total.astype(BF)

        loop(0, Z, sum_y)

        def send(d):
            zz = lax.rem(z + d, Z)
            remote(
                sy.at[c, zz], rz.at[c, d - 1], s_rs.at[11 + Y, c], r_rs.at[11 + Y, c], (dp, zz * Y + y)
            ).start()

        loop(1, Z, send)

    def rs_z_desc(c):
        return remote(rz.at[c], rz.at[c], s_rs.at[11 + Y, c], r_rs.at[11 + Y, c], pdev)

    def rs_sum(c):
        rs_z_desc(c).wait_recv()
        total = sy[c, z].astype(F32)
        for d in range(Z - 1):
            total = total + rz[c, d].astype(F32)
        fin[:, cols(c)] = total.astype(BF)

    def field_rows(c):
        a2a_desc(3, c).wait_recv()
        front = mm(a4[...], got(3, c)) + skip[:, mine(c)] * p[c].reshape(M, CW).astype(F32)
        pgo[c] = front.astype(BF).reshape(2, rows, CW)

    out_pre = [local(pgo.at[c, h], pre.at[:, mine(c)], 4 + NC + c) for c in range(NC)]
    c_pre = [
        remote(pgo.at[c, other], pre.at[:, mine(c)], s_pair.at[NC + 2 + c], r_pair.at[NC + 2 + c], pdev)
        for c in range(NC)
    ]

    in_kern.wait()
    for c in range(NC):
        back_columns(c)
        a2a_start_odd(1, c)
        ag_x2(c)
        a2a_start_even(1, c)
    in_tok.wait()
    c_tok.wait_recv()
    project(0)

    a2a_desc(1, 0).wait_recv()
    a2a_start_odd(2, 0)
    gradient_rows(0)
    rs_x1(0)
    a2a_start_even(2, 0)
    for c in range(1, NC):
        project(c)
        rs_x2(c - 1)
        a2a_desc(1, c).wait_recv()
        a2a_start_odd(2, c)
        gradient_rows(c)
        rs_x1(c)
        a2a_start_even(2, c)

    def token_rows(i, b):
        total = mm_tb(gp[0, b], wb[0, i].reshape(TI, CW))
        for c in range(1, NC):
            total = total + mm_tb(gp[c, b], wb[c, i].reshape(TI, CW))
        return total.astype(BF)

    def gt_other(i):
        gts[:, pl.ds(pl.multiple_of(i * TI, TI), TI)] = token_rows(i, other)

    loop(0, Z, gt_other)
    c_gt = remote(gts, gtr, s_pair.at[NC + 1], r_pair.at[NC + 1], pdev)
    c_gt.start()

    rs_x3(0)
    forward_columns(0)
    rs_x2(NC - 1)
    a2a_start_odd(3, 0)
    rs_y(0)
    a2a_start_even(3, 0)
    rs_x3(NC - 1)

    def gt_own(i):
        gto[:, pl.ds(pl.multiple_of(i * TI, TI), TI)] = token_rows(i, h)

    loop(0, Z, gt_own)
    out_gt = local(gto, gtown, 4 + 2 * NC)
    out_gt.start()

    for c in range(1, NC):
        forward_columns(c)
        rs_z(c - 1)
        a2a_start_odd(3, c)
        rs_y(c)
    a2a_start_even(3, NC - 1)

    for c in range(NC - 1):
        rs_sum(c)
        field_rows(c)
        out_pre[c].start()
        c_pre[c].start()
    rs_z(NC - 1)
    field_rows(NC - 1)
    out_pre[NC - 1].start()
    c_pre[NC - 1].start()
    rs_sum(NC - 1)
    my_rows = gfin.at[dp]

    def share(d):
        remote(fin, my_rows, s_rs.at[12 + Y, 0], r_rs.at[12 + Y, 0], (lax.rem(dp + d, DP), k)).start()

    loop(1, DP, share)
    out_fin = local(fin, my_rows, 5 + 2 * NC)
    out_fin.start()
    share_desc = remote(
        gfin.at[pl.ds(0, DP - 1)], gfin.at[pl.ds(0, DP - 1)], s_rs.at[12 + Y, 0], r_rs.at[12 + Y, 0], pdev
    )

    for c in range(NC):
        out_pre[c].wait()
        c_pre[c].wait()
        c_g[c].wait_send()
        for copy in (c_xr2[c], c_xl2[c], ag_z_desc(c)):
            copy.wait_send()
        for d in range(Y):
            for copy in ag_x1_copies(c, d):
                copy.wait_send()
        for d in near:
            ag_y_copy(c, d).wait_send()
        for copy in rs_copies(c, False) + rs_copies(c, True):
            copy.wait_send()
        for d in near:
            rs_y_copy(c, d).wait_send()
        rs_z_desc(c).wait_send()
        for ph in range(4):
            a2a_desc(ph, c).wait_send()
    c_tok.wait_send()
    c_gt.wait()
    out_gt.wait()
    out_fin.wait()
    share_desc.wait()


def finish(pre, gate, cot, gtown, gtr, gfin, mixed, gtok, ggate, gwt, mv, tv, gv, wv, sems):
    rows, D = pre.shape
    HC = gfin.shape[2]
    part = rows // X
    copies = []
    for i in range(X):
        r = slice(i * part, (i + 1) * part)
        at = pl.ds(i * part, part)
        front = pre[r].astype(F32)
        mv[r] = (gate[r].astype(F32) * front).astype(BF)
        copies.append(pltpu.make_async_copy(mv.at[at], mixed.at[at], sems.at[4 * i]))
        copies[-1].start()
        gv[r] = (cot[r].astype(F32) * front).astype(BF)
        copies.append(pltpu.make_async_copy(gv.at[at], ggate.at[at], sems.at[4 * i + 1]))
        copies[-1].start()
        tv[r] = (gtown[r].astype(F32) + gtr[r].astype(F32)).astype(BF)
        copies.append(pltpu.make_async_copy(tv.at[at], gtok.at[at], sems.at[4 * i + 2]))
        copies[-1].start()
        for j in range(2):
            wv[i, :, j * HC:(j + 1) * HC] = gfin[2 * i + j].astype(F32)
        copies.append(pltpu.make_async_copy(wv.at[i], gwt.at[i], sems.at[4 * i + 3]))
        copies[-1].start()
    for copy in copies:
        copy.wait()


def per_device(Y, CTX, tokens, weight, gate, skip, first, second, kern, third, fourth, cotangent):
    _, rows, D = tokens.shape
    HC = D // 2
    CW = HC // NC
    Z = CTX // Y
    M = 2 * rows
    CH = M // CTX
    R = first.shape[1]
    SL, Q = second.shape[0], second.shape[1]
    WR = D // CTX // X
    vm = pl.BlockSpec(memory_space=pltpu.VMEM)
    hbm = pl.BlockSpec(memory_space=pl.ANY)
    pre, gtown, gtr, gfin = pl.pallas_call(
        functools.partial(kernel, Y),
        out_shape=(
            pltpu.VMEM((rows, D), BF),
            pltpu.VMEM((rows, D), BF),
            pltpu.VMEM((rows, D), BF),
            pltpu.VMEM((2 * X, WR, HC), BF),
        ),
        in_specs=[hbm] * 10,
        out_specs=(vm,) * 4,
        scratch_shapes=[
            pltpu.VMEM((first.shape[0], R, R), BF),
            pltpu.VMEM((SL, Q, Q), BF),
            pltpu.VMEM((SL, Q, Q), BF),
            pltpu.VMEM((first.shape[0], R, R), BF),
            pltpu.VMEM((1, D), F32),
            pltpu.VMEM((M, M), BF),
            pltpu.VMEM((rows, D), BF),
            pltpu.VMEM((rows, D), BF),
            pltpu.VMEM((rows, D), BF),
            pltpu.VMEM((rows, D), BF),
            pltpu.VMEM((Q, SL, HC), BF),
            pltpu.VMEM((NC, 2, rows, CW), BF),
            pltpu.VMEM((NC, rows, CW), BF),
            pltpu.VMEM((NC, 2, rows, CW), BF),
            pltpu.VMEM((NC, 2, rows, CW), BF),
            pltpu.VMEM((NC, Z, Y, X, WR, CW), BF),
            pltpu.VMEM((NC, Z, Y, X, WR, CW), BF),
            pltpu.VMEM((4, NC, CTX, CH, CW), BF),
            pltpu.VMEM((4, NC, CTX, CH, CW), BF),
            pltpu.VMEM((NC, 2, Z // 2, Y, WR, CW), BF),
            pltpu.VMEM((NC, 2, Z, Y, WR, CW), BF),
            pltpu.VMEM((NC, Z, Y, WR, CW), BF),
            pltpu.VMEM((NC, Y - 1, Z, WR, CW), BF),
            pltpu.VMEM((NC, Z, WR, CW), BF),
            pltpu.VMEM((NC, Z - 1, WR, CW), BF),
            pltpu.VMEM((WR, HC), BF),
            pltpu.VMEM((M, M), BF),
            pltpu.VMEM((M, M), BF),
            pltpu.VMEM((M, M), BF),
            pltpu.VMEM((M, M), BF),
            pltpu.VMEM((SL * Q, M), BF),
            pltpu.VMEM((rows, D), BF),
            pltpu.VMEM((rows, D), BF),
            pltpu.VMEM((NC, 2, rows, CW), BF),
            pltpu.SemaphoreType.DMA((3 * Y + 2, NC)),
            pltpu.SemaphoreType.DMA((3 * Y + 2, NC)),
            pltpu.SemaphoreType.DMA((2 * NC + 2,)),
            pltpu.SemaphoreType.DMA((2 * NC + 2,)),
            pltpu.SemaphoreType.DMA((4, NC)),
            pltpu.SemaphoreType.DMA((4, NC)),
            pltpu.SemaphoreType.DMA((13 + Y, NC)),
            pltpu.SemaphoreType.DMA((13 + Y, NC)),
            pltpu.SemaphoreType.DMA((2 * NC + 11,)),
        ],
        compiler_params=pltpu.CompilerParams(
            collective_id=0, has_side_effects=True, vmem_limit_bytes=52 * 1024 * 1024
        ),
        cost_estimate=pl.CostEstimate(
            flops=8 * rows * D * D, bytes_accessed=8 * rows * D * 2, transcendentals=0
        ),
    )(
        tokens[0],
        weight.reshape(X, WR, D),
        gate[0],
        skip.reshape(1, D),
        first,
        second,
        kern,
        third,
        fourth,
        cotangent[0],
    )
    mixed, gtok, ggate, gwt = pl.pallas_call(
        finish,
        out_shape=(
            jax.ShapeDtypeStruct((rows, D), BF),
            jax.ShapeDtypeStruct((rows, D), BF),
            jax.ShapeDtypeStruct((rows, D), BF),
            jax.ShapeDtypeStruct((X, WR, D), F32),
        ),
        in_specs=[vm] * 6,
        out_specs=(hbm,) * 4,
        scratch_shapes=[
            pltpu.VMEM((rows, D), BF),
            pltpu.VMEM((rows, D), BF),
            pltpu.VMEM((rows, D), BF),
            pltpu.VMEM((X, WR, D), F32),
            pltpu.SemaphoreType.DMA((4 * X,)),
        ],
        compiler_params=pltpu.CompilerParams(vmem_limit_bytes=16 * 1024 * 1024),
        cost_estimate=pl.CostEstimate(
            flops=8 * rows * D, bytes_accessed=16 * rows * D, transcendentals=0
        ),
    )(pre, gate[0], cotangent[0], gtown, gtr, gfin)
    return mixed[None], gtok[None], ggate[None], gwt.reshape(X * WR, D)


def solution(mesh, y_size=4):
    in_specs = (
        P("dp", "context", None),
        P("context", None),
        P("dp", "context", None),
        P(),
        P("context", None, None),
        P("context", None, None),
        P(None, "context", None),
        P("context", None, None),
        P("context", None, None),
        P("dp", "context", None),
    )
    out_specs = (
        P("dp", "context", None),
        P("dp", "context", None),
        P("dp", "context", None),
        P("context", None),
    )
    return jax.shard_map(
        functools.partial(per_device, y_size, mesh.shape["context"]),
        mesh=mesh, in_specs=in_specs, out_specs=out_specs, check_vma=False,
    )
```
